256 devices in a mesh: expert: 128 (over z, y, x), section: 2 (over core).
Axes of the slice: x: 4, y: 4, z: 8, core: 2. Of those that a mesh axis runs over, the one named last changes fastest.
Arguments:
- tokens: bfloat16 [2048, 2048], P('expert'), may hold values from -6 to 6
- routes: int32 [2048, 8], P('expert'), may hold values from 0 to 127, all different within a row; in each aligned block of 16 rows (0 to 15, 16 to 31, ...) at most 2 rows name the same one
- route_weight: float32 [2048, 8], P('expert'), may hold values from 0.1 to 1
- moe_gain: float32 [2048], replicated, may hold values from 0.5 to 1.5
- expert_gate: bfloat16 [128, 2048, 768], P('expert', None, 'section'), may hold values from -0.125 to 0.125
- expert_up: bfloat16 [128, 2048, 768], P('expert', None, 'section'), may hold values from -0.125 to 0.125
- expert_down: bfloat16 [128, 768, 2048], P('expert', 'section'), may hold values from -0.21875 to 0.21875
- talker_proj: bfloat16 [2048, 1024], P('section'), may hold values from -0.125 to 0.125
- codebook_table: bfloat16 [2, 2048, 1024], P('section'), may hold values from -6 to 6
- level_gain: float32 [2, 1024], P('section'), may hold values from 0.5 to 1.5
- earlier_codes: int32 [2048], P('expert'), may hold values from 0 to 2047
Outputs:
- hidden_out: bfloat16 [2048, 2048], P('expert', 'section')
- logits: bfloat16 [2048, 2, 2048], P('expert', 'section')
The draws below stay inside these ranges and needn't reach their ends.
Inputs may be any that keep to these rules, and one draw needn't show every extreme that they name: Among the rows of one index of expert, no expert is named by more than 2 of the 8 routes of its tokens, and some expert reaches 2; a token names 8 different experts.
All inputs are finite; a program needn't handle non-finite values.
Results may differ from the reference program's by a relative error of at most 0.012.
Values may be sent and summed in bfloat16 or wider, within the bound.
A program may use at most 64 MiB of HBM per device.

```python
import math
import jax
import jax.numpy as jnp
import numpy as np
from jax import lax

D = 2048
MOE_FF = 768
TOP = 8
TD = 1024
V = 2048
TOK_DEV = 16
EXPERTS = 128
TOKENS = 2048
CAP = 2
LEVELS = 2
N_EXPERT = 128


def set_ends(values, rng, least, high):
    longest = values.shape.index(max(values.shape))
    spots = []
    for shift in (0, 1):
        where = [jax.random.randint(jax.random.fold_in(rng, axis), (), 0, length) for axis, length in enumerate(values.shape)]
        where[longest] = (where[longest] + shift) % values.shape[longest]
        spots.append(tuple(where))
    return values.at[spots[0]].set(least).at[spots[1]].set(high)


def block_scale(rng, shape, cuts, low, top_value):
    level, own = 1.0, jax.random.fold_in(rng, 6)
    for axis_at, blocks in cuts:
        steps = jnp.exp(jax.random.uniform(jax.random.fold_in(own, axis_at), (blocks,), jnp.float32, low / len(cuts), top_value / len(cuts)))
        level = level * jnp.repeat(steps, shape[axis_at] // blocks).reshape([-1 if axis == axis_at else 1 for axis in range(len(shape))])
    return level


def rank_bounds(count, lean):
    loads = [(1 << 20) // math.isqrt(grade ** lean) + 1 for grade in range(1, count + 1)]
    deviation = 1 + sum(loads) // (1 << 30)
    return np.cumsum(np.array([max(1, weight // deviation) for weight in loads]))


def skewed_ids(rng, shape, count, lean):
    listing = rank_bounds(count, lean)
    lot = jax.random.randint(jax.random.fold_in(rng, 1), shape, 0, int(listing[count - 1]))
    standing = jnp.searchsorted(jnp.asarray(listing, jnp.int32), lot, side="right")
    return jax.random.permutation(jax.random.fold_in(rng, 2), count)[standing].astype(jnp.int32)


def assign_block(stream_key, own, number, rows, count, top, most, slope):
    order = jax.random.permutation(stream_key, count)
    crowded, ordinary = load_shares(count, rows * top, most, slope, True), load_shares(count, rows * top, most, slope, False)
    places = jnp.arange(count)

    def named(tallies, turn):
        used = int((tallies > 0).sum())
        fixed = max(1, used // 4)
        passed = fixed + (places - fixed + turn * (used - fixed)) % max(1, count - fixed)
        return jnp.zeros((count,), jnp.int32).at[order[jnp.where(places < fixed, places, passed)]].set(jnp.asarray(tallies, jnp.int32))

    tallies = jnp.where(number % 4 == 0, named(crowded, number // 4), named(ordinary, number - number // 4 - 1))
    mixed = jax.random.permutation(jax.random.fold_in(own, 3), count)
    source_of, taker = mixed[0:count // 2 * 2:2], mixed[1:count // 2 * 2:2]
    margin = jnp.minimum(tallies[source_of] - 1, most - tallies[taker]) // 2
    margin = jnp.where((source_of == order[0]) | (taker == order[0]) | (tallies[taker] == 0), 0, jnp.maximum(margin, 0))
    passed = jax.random.randint(jax.random.fold_in(own, 4), (count // 2,), 0, 1 << 20) % (margin + 1)
    tallies = tallies.at[source_of].add(-passed).at[taker].add(passed)
    items = jnp.searchsorted(jnp.cumsum(tallies), jnp.arange(rows * top), side="right").astype(jnp.int32)
    listing = items.reshape(top, rows).T
    listing = listing[jax.random.permutation(jax.random.fold_in(own, 1), rows)]
    turn = jax.random.randint(jax.random.fold_in(own, 2), (rows, 1), 0, top)
    return jnp.take_along_axis(listing, (jnp.arange(top)[None, :] + turn) % top, axis=1)


def load_shares(number_of, total, most, lean, full):
    weights = [(1 << 20) // math.isqrt(rank ** lean) + 1 for rank in range(1, number_of + 1)]
    largest = most if full else min(most, max(-(-total // number_of), total * weights[0] // sum(weights)))
    least = 1 if total - largest >= number_of - 1 else 0
    given, rest = [largest] + [least] * (number_of - 1), total - largest - least * (number_of - 1)
    while rest > 0:
        candidates = [i for i in range(1, number_of) if given[i] < largest] or [i for i in range(1, number_of) if given[i] < most]
        pool, budget = sum([weights[i] for i in candidates]), rest
        for i in candidates:
            addition = min(most - given[i], max(1, budget * weights[i] // pool), rest)
            given[i] = given[i] + addition
            rest = rest - addition
    return np.array(given)


def centred(rng, shape, deviation, most, cuts=(), kind=jnp.bfloat16):
    drawn = jax.random.normal(rng, shape, jnp.float32) * deviation
    if len(cuts) > 0:
        drawn = block_scale(rng, shape, cuts, -0.22, 0.18) * drawn
    return jnp.clip(drawn, min=-most, max=most).astype(kind)


def setup_inputs(seed: int = 0) -> dict:
    keys = jax.random.split(jax.random.key(seed), 12)
    tokens = centred(keys[0], (TOKENS, D), 1.0, 6.0, ((0, 128),))
    routes_keys = jax.random.split(jax.random.fold_in(keys[1], 1), TOKENS // TOK_DEV)
    routes_turns = jax.random.permutation(jax.random.fold_in(keys[1], 3), TOKENS // TOK_DEV)
    routes = jax.vmap(lambda own, number: assign_block(jax.random.fold_in(keys[1], 2), own, number, TOK_DEV, EXPERTS, TOP, CAP, 2))(routes_keys, routes_turns).reshape((TOKENS, TOP))
    route_weight = jnp.clip(jnp.exp(math.log(1.0) - 2.3025851 * jax.random.uniform(keys[2], (TOKENS, TOP), jnp.float32) ** block_scale(keys[2], (TOKENS, TOP), ((0, 128),), -0.2, 0.2)), 0.1, 1.0)
    moe_gain = jnp.clip(1.0 + 0.1 * jax.random.normal(keys[3], (D,), jnp.float32), 0.5, 1.5)
    expert_gate = centred(keys[4], (EXPERTS, D, MOE_FF), D ** -0.5, 0.125, ((0, 128), (2, 2)))
    expert_up = centred(keys[5], (EXPERTS, D, MOE_FF), D ** -0.5, 0.125, ((0, 128), (2, 2)))
    expert_down = centred(keys[6], (EXPERTS, MOE_FF, D), MOE_FF ** -0.5, 0.21875, ((0, 128), (1, 2)))
    talker_proj = centred(keys[7], (D, TD), D ** -0.5, 0.125, ((0, 2),))
    codebook_table = centred(keys[8], (LEVELS, V, TD), 1.0, 6.0, ((0, 2),))
    level_gain = jnp.clip(1.0 + 0.1 * jax.random.normal(keys[9], (LEVELS, TD), jnp.float32), 0.5, 1.5)
    earlier_codes = set_ends(skewed_ids(keys[10], (TOKENS,), V, 2), jax.random.fold_in(keys[10], 3), 0, V - 1).astype(jnp.int32)
    return dict(tokens=tokens, routes=routes, route_weight=route_weight, moe_gain=moe_gain, expert_gate=expert_gate, expert_up=expert_up, expert_down=expert_down, talker_proj=talker_proj, codebook_table=codebook_table, level_gain=level_gain, earlier_codes=earlier_codes)


def rms_scale(values, gain_row):
    mean_square = lax.optimization_barrier(jnp.mean(values * values, axis=-1, keepdims=True)) + 1e-06
    return values * lax.rsqrt(mean_square) * gain_row

def reference(tokens, routes, route_weight, moe_gain, expert_gate, expert_up, expert_down, talker_proj, codebook_table, level_gain, earlier_codes):
    normed = rms_scale(tokens.astype(jnp.float32), moe_gain).astype(jnp.bfloat16)
    shares = route_weight / lax.optimization_barrier(jnp.sum(route_weight, axis=1, keepdims=True))
    route_flat = routes.reshape(-1).astype(jnp.int32)
    share_flat = shares.reshape(-1)
    ordering = jnp.argsort(route_flat, stable=True).astype(jnp.int32)
    expert_ids = jnp.arange(EXPERTS, dtype=jnp.int32)
    counts = lax.optimization_barrier(jnp.sum((route_flat[:, None] == expert_ids[None, :]).astype(jnp.int32), axis=0)).astype(jnp.int32)
    starts = (jnp.cumsum(counts) - counts).astype(jnp.int32)
    row_limit = N_EXPERT * CAP
    padded_order = jnp.concatenate([ordering, jnp.zeros((row_limit,), jnp.int32)])

    def expert_step(carry_sum, packed):
        gate_w, up_w, down_w, begin, count = packed
        picked = lax.dynamic_slice_in_dim(padded_order, begin.astype(jnp.int32), row_limit)
        valid = jnp.arange(row_limit, dtype=jnp.int32) < count
        token_rows = (picked // TOP).astype(jnp.int32)
        rows_in = normed[token_rows]
        gate_val = jnp.dot(rows_in, gate_w, preferred_element_type=jnp.float32)
        up_val = jnp.dot(rows_in, up_w, preferred_element_type=jnp.float32)
        hidden_units = (jax.nn.silu(gate_val) * up_val).astype(jnp.bfloat16)
        outputs = jnp.dot(hidden_units, down_w, preferred_element_type=jnp.float32)
        outputs = lax.optimization_barrier(outputs.astype(jnp.bfloat16)).astype(jnp.float32)
        weights_row = jnp.where(valid, share_flat[picked], jnp.zeros_like(share_flat[picked]))
        carry_sum = carry_sum.at[token_rows].add(outputs * weights_row[:, None])
        return (carry_sum, None)
    mixture, _ = lax.scan(expert_step, jnp.zeros((TOKENS, D), jnp.float32), (expert_gate, expert_up, expert_down, starts, counts))
    hidden_out = (tokens.astype(jnp.float32) + mixture).astype(jnp.bfloat16)
    talk = jnp.dot(hidden_out, talker_proj, preferred_element_type=jnp.float32)
    second = talk + codebook_table[0][earlier_codes].astype(jnp.float32)
    level_inputs = [talk, second]
    level_logits = []
    for level in range(2):
        level_normed = rms_scale(level_inputs[level], level_gain[level]).astype(jnp.bfloat16)
        scores = lax.dot_general(level_normed, codebook_table[level], (((1,), (1,)), ((), ())), preferred_element_type=jnp.float32)
        level_logits.append(scores / math.sqrt(TD))
    logits = jnp.stack(level_logits, axis=1).astype(jnp.bfloat16)
    return (hidden_out, logits)
```

```python
import functools

import jax
import jax.numpy as jnp
from jax import lax
from jax.experimental import pallas as pl
from jax.experimental.pallas import tpu as pltpu
from jax.sharding import PartitionSpec as P

MESH = pl.DeviceIdType.MESH
NZ, NY, NX = 8, 4, 4
CAP = 2
CHUNKS = 2
GROUPS = 4
META = 128
BF, F32 = jnp.bfloat16, jnp.float32


def kernel(
    tokens_hbm, routes_hbm, weight_hbm, gain_hbm, gate_hbm, up_hbm, down_hbm, proj_hbm, table_hbm, lgain_hbm, codes,
    hidden_out, logits_out,
    tok, rts, rwt, gain, lgain, wgu, wd, wp, tb,
    zbuf, sel, recv, part, acc, psend, precv, own, outb, ret, zout, zin, wmix, emb, tsend, trecv,
    load_sem, z_s, z_r, p_s, p_r, f_s, f_r, q_s, q_r, r_s, r_r, u_s, u_r, t_s, t_r,
):
    plane = NY * NX
    rows, width = tok.shape
    half = width // 2
    ff = gate_hbm.shape[2]
    top = rts.shape[1]
    experts = NZ * plane
    cw = half // CHUNKS
    slots = plane * NZ * CAP
    span = NZ * CAP
    stream = NZ * rows
    me = lax.axis_index("expert")
    sec = lax.axis_index("section")
    x, y, z = me % NX, (me // NX) % NY, me // plane
    other = 1 - sec

    def at_plane(dy, dx):
        return z * plane + ((y + dy) % NY) * NX + (x + dx) % NX

    def at_z(dz):
        return ((z + dz) % NZ) * plane + y * NX + x

    forth = [(o, at_plane(o // NX, o % NX)) for o in range(1, plane)]
    back = [(o, at_plane(NY - o // NX, NX - o % NX)) for o in range(1, plane)]

    pairs = [
        (tokens_hbm, tok),
        (routes_hbm, rts),
        (weight_hbm, rwt),
        (gain_hbm, gain),
        (lgain_hbm, lgain),
        (gate_hbm.at[0, pl.ds(sec * half, half), :], wgu.at[0, :, 0:ff]),
        (up_hbm.at[0, pl.ds(sec * half, half), :], wgu.at[0, :, ff : 2 * ff]),
        (gate_hbm.at[0, pl.ds(other * half, half), :], wgu.at[1, :, 0:ff]),
        (up_hbm.at[0, pl.ds(other * half, half), :], wgu.at[1, :, ff : 2 * ff]),
        (down_hbm.at[0, :, pl.ds(other * half, half)], wd.at[1]),
        (down_hbm.at[0, :, pl.ds(sec * half, half)], wd.at[0]),
        (table_hbm.at[0], tb),
        (proj_hbm, wp),
    ]
    loads = [pltpu.make_async_copy(src, dst, load_sem.at[i]) for i, (src, dst) in enumerate(pairs)]
    for load in loads:
        load.start()

    barrier = pltpu.get_barrier_semaphore()
    for d in range(1, NZ):
        pl.semaphore_signal(barrier, inc=1, device_id=(at_z(d), sec), device_id_type=MESH)
    for _, peer in forth:
        pl.semaphore_signal(barrier, inc=1, device_id=(peer, sec), device_id_type=MESH)
    pl.semaphore_signal(barrier, inc=1, device_id=(me, other), device_id_type=MESH)

    for i in range(4):
        loads[i].wait()
    routes = rts[...]
    expert_lane = lax.broadcasted_iota(jnp.int32, (rows, experts), 1)
    named = [routes[:, k : k + 1] == expert_lane for k in range(top)]
    hit = functools.reduce(jnp.logical_or, named)
    below = lax.broadcasted_iota(jnp.int32, (rows, rows), 0) > lax.broadcasted_iota(jnp.int32, (rows, rows), 1)
    earlier = jnp.dot(below.astype(F32).astype(BF), hit.astype(F32).astype(BF), preferred_element_type=F32)
    weight = rwt[...]
    shares = weight / jnp.sum(weight, axis=1, keepdims=True)
    shares_hi = shares.astype(BF).astype(F32)
    shares_lo = shares - shares_hi
    lane = lax.broadcasted_iota(jnp.int32, (rows, META), 1)
    meta = jnp.zeros((rows, META), F32)
    for k in range(top):
        rank = jnp.sum(jnp.where(named[k], earlier, 0.0), axis=1, keepdims=True)
        target = routes[:, k : k + 1].astype(F32) * CAP + rank
        meta = jnp.where(lane == k, target, meta)
        meta = jnp.where(lane == top + k, shares_hi[:, k : k + 1], meta)
        meta = jnp.where(lane == 2 * top + k, shares_lo[:, k : k + 1], meta)
    zbuf[0, :, 0:META] = meta.astype(BF)
    values = tok[...].astype(F32)
    scale = lax.rsqrt(jnp.mean(values * values, axis=1, keepdims=True) + 1e-06)
    mine = tok[:, pl.ds(sec * half, half)].astype(F32)
    zbuf[0, :, META:] = (mine * scale * gain[:, pl.ds(sec * half, half)]).astype(BF)

    pl.semaphore_wait(barrier, NZ - 1 + plane - 1 + 1)

    def z_lanes(c):
        return pl.ds(0, META + cw) if c == 0 else pl.ds(META + c * cw, cw)

    def z_copy(c, src, dst, device):
        return pltpu.make_async_remote_copy(
            src_ref=zbuf.at[src, :, z_lanes(c)], dst_ref=zbuf.at[dst, :, z_lanes(c)],
            send_sem=z_s.at[c], recv_sem=z_r.at[c], device_id=(device, sec), device_id_type=MESH,
        )

    for c in range(CHUNKS):
        for d in range(1, NZ):
            z_copy(c, 0, d, at_z(d)).start()

    slot = lax.broadcasted_iota(jnp.int32, (slots, 1), 0)
    slot_o, slot_d, slot_s = slot // span, (slot // CAP) % NZ, slot % CAP
    slot_expert = z * plane + ((y + slot_o // NX) % NY) * NX + (x + slot_o % NX) % NX
    slot_target = (slot_expert * CAP + slot_s).astype(F32)
    same_block = slot_d == lax.broadcasted_iota(jnp.int32, (slots, stream), 1) // rows

    def plane_copy(c, src, dst, peer, o, send, get):
        return pltpu.make_async_remote_copy(
            src_ref=src.at[c, o], dst_ref=dst.at[c, o], send_sem=send, recv_sem=get,
            device_id=(peer, sec), device_id_type=MESH,
        )

    per = plane // GROUPS
    for c in range(CHUNKS):
        z_copy(c, pl.ds(1, NZ - 1), pl.ds(1, NZ - 1), me).wait_recv()
        if c == 0:
            columns = zbuf[:, :, 0:META].reshape(stream, META).astype(F32)
            across = columns.T
            pick = functools.reduce(jnp.logical_or, [across[k : k + 1, :] == slot_target for k in range(top)])
            pick = jnp.logical_and(pick, same_block).astype(F32).astype(BF)
        features = zbuf[:, :, META + c * cw : META + (c + 1) * cw].reshape(stream, cw)
        chosen = jnp.dot(pick, features, preferred_element_type=F32).astype(BF).reshape(plane, span, cw)
        sel[c] = chosen
        recv[c, 0] = chosen[0]
        for o, peer in forth:
            plane_copy(c, sel, recv, peer, o, p_s.at[c], p_r.at[c, o // per]).start()

    lane_slot = lax.broadcasted_iota(jnp.int32, (1, slots), 1)
    lane_o = lane_slot // span
    lane_expert = z * plane + ((y + lane_o // NX) % NY) * NX + (x + lane_o % NX) % NX
    lane_target = (lane_expert * CAP + lane_slot % CAP).astype(F32)
    lane_block = (lane_slot // CAP) % NZ == lax.broadcasted_iota(jnp.int32, (stream, slots), 0) // rows
    hi = jnp.zeros((stream, slots), F32)
    lo = jnp.zeros((stream, slots), F32)
    for k in range(top):
        here = jnp.logical_and(columns[:, k : k + 1] == lane_target, lane_block)
        hi = jnp.where(here, columns[:, top + k : top + k + 1], hi)
        lo = jnp.where(here, columns[:, 2 * top + k : 2 * top + k + 1], lo)
    wmix[0:stream] = hi.astype(BF)
    wmix[stream:] = lo.astype(BF)

    vocabulary = tb.shape[0]
    column = jnp.zeros((rows, 1), jnp.int32)
    row_at = lax.broadcasted_iota(jnp.int32, (rows, 1), 0)
    for i in range(rows):
        column = jnp.where(row_at == i, codes[i], column)
    code_hit = (column == lax.broadcasted_iota(jnp.int32, (rows, vocabulary), 1)).astype(F32).astype(BF)
    loads[11].wait()
    emb[...] = jnp.dot(code_hit, tb[...], preferred_element_type=F32)

    def core_copy(src, dst, send, get):
        return pltpu.make_async_remote_copy(
            src_ref=src, dst_ref=dst, send_sem=send, recv_sem=get, device_id=(me, other), device_id_type=MESH
        )

    for i in range(5, 9):
        loads[i].wait()
    for c in range(CHUNKS):
        for g in range(GROUPS):
            block = pl.ds(max(g * per, 1), (g + 1) * per - max(g * per, 1))
            plane_copy(c, sel, recv, me, block, p_s.at[c], p_r.at[c, g]).wait_recv()
            group = pl.ds(g * per, per)
            core_copy(recv.at[c, group], part.at[c, group], f_s.at[c], f_r.at[c]).start()
        product = jnp.dot(recv[c].reshape(slots, cw), wgu[0, c * cw : (c + 1) * cw, :], preferred_element_type=F32)
        acc[...] = product if c == 0 else acc[...] + product
    for c in range(CHUNKS):
        core_copy(recv.at[c], part.at[c], f_s.at[c], f_r.at[c]).wait_recv()
        acc[...] += jnp.dot(part[c].reshape(slots, cw), wgu[1, c * cw : (c + 1) * cw, :], preferred_element_type=F32)
    gate_val = acc[:, 0:ff]
    units = (gate_val / (1.0 + jnp.exp(-gate_val)) * acc[:, ff:]).astype(BF)

    loads[9].wait()
    for c in range(CHUNKS):
        partial = jnp.dot(units, wd[1, :, c * cw : (c + 1) * cw], preferred_element_type=F32)
        psend[c] = partial.astype(BF)
        core_copy(psend.at[c], precv.at[c], q_s.at[c], q_r.at[c]).start()
    loads[10].wait()
    for c in range(CHUNKS):
        own[c] = jnp.dot(units, wd[0, :, c * cw : (c + 1) * cw], preferred_element_type=F32)
    for c in range(CHUNKS):
        core_copy(psend.at[c], precv.at[c], q_s.at[c], q_r.at[c]).wait_recv()
        finished = (own[c] + precv[c].astype(F32)).astype(BF).reshape(plane, span, cw)
        outb[c] = finished
        ret[c, 0] = finished[0]
        for o, peer in back:
            plane_copy(c, outb, ret, peer, o, r_s.at[c], r_r.at[c]).start()

    for c in range(CHUNKS):
        z_copy(c, pl.ds(1, NZ - 1), pl.ds(1, NZ - 1), me).wait_send()
        plane_copy(c, sel, recv, me, pl.ds(1, plane - 1), p_s.at[c], p_r.at[c, 0]).wait_send()
        core_copy(recv.at[c], part.at[c], f_s.at[c], f_r.at[c]).wait_send()

    def u_copy(c, d, device):
        return pltpu.make_async_remote_copy(
            src_ref=zout.at[c, d], dst_ref=zin.at[c, d], send_sem=u_s.at[c], recv_sem=u_r.at[c],
            device_id=(device, sec), device_id_type=MESH,
        )

    everyone = pl.ds(1, plane - 1)
    for c in range(CHUNKS):
        plane_copy(c, outb, ret, me, everyone, r_s.at[c], r_r.at[c]).wait_recv()
        both = jnp.dot(wmix[...], ret[c].reshape(slots, cw), preferred_element_type=F32)
        summed = (both[0:stream] + both[stream:]).astype(BF).reshape(NZ, rows, cw)
        zout[c] = summed
        zin[c, 0] = summed[0]
        for d in range(1, NZ):
            u_copy(c, d, at_z(NZ - d)).start()

    loads[12].wait()
    loads[4].wait()
    partial_talk = None
    for c in range(CHUNKS):
        u_copy(c, pl.ds(1, NZ - 1), me).wait_recv()
        mixture = functools.reduce(jnp.add, [zin[c, d].astype(F32) for d in range(NZ)])
        at = pl.multiple_of(sec * half + c * cw, cw)
        complete = (tok[:, pl.ds(at, cw)].astype(F32) + mixture).astype(BF)
        hidden_out[:, c * cw : (c + 1) * cw] = complete
        product = jnp.dot(complete, wp[c * cw : (c + 1) * cw, :], preferred_element_type=F32)
        partial_talk = product if partial_talk is None else partial_talk + product
    tsend[...] = partial_talk + jnp.where(sec == 0, emb[...], 0.0)
    talk_copy = core_copy(tsend, trecv, t_s, t_r)
    talk_copy.start()
    for c in range(CHUNKS):
        core_copy(psend.at[c], precv.at[c], q_s.at[c], q_r.at[c]).wait_send()
        plane_copy(c, outb, ret, me, everyone, r_s.at[c], r_r.at[c]).wait_send()
        u_copy(c, pl.ds(1, NZ - 1), me).wait_send()
    talk_copy.wait()

    level = partial_talk + trecv[...]
    level_scale = lax.rsqrt(jnp.mean(level * level, axis=1, keepdims=True) + 1e-06)
    level_normed = (level * level_scale * lgain[...]).astype(BF)
    scores = lax.dot_general(level_normed, tb[...], (((1,), (1,)), ((), ())), preferred_element_type=F32)
    logits_out[...] = (scores / (level.shape[1] ** 0.5)).astype(BF)


def shards(
    tokens,
    routes,
    route_weight,
    moe_gain,
    expert_gate,
    expert_up,
    expert_down,
    talker_proj,
    codebook_table,
    level_gain,
    earlier_codes,
):
    rows, width = tokens.shape
    top = routes.shape[1]
    half, plane = width // 2, NY * NX
    ff = expert_gate.shape[2]
    vocabulary, talk_width = codebook_table.shape[1:]
    cw = half // CHUNKS
    span, stream = NZ * CAP, NZ * rows
    slots = plane * span
    chunk = (CHUNKS, plane, span, cw)
    dma = pltpu.SemaphoreType.DMA
    anywhere = pl.BlockSpec(memory_space=pl.ANY)
    vmem = pl.BlockSpec(memory_space=pltpu.VMEM)
    hidden, logits = pl.pallas_call(
        kernel,
        out_shape=(
            jax.ShapeDtypeStruct((rows, half), BF),
            jax.ShapeDtypeStruct((rows, vocabulary), BF),
        ),
        in_specs=[anywhere] * 10 + [pl.BlockSpec(memory_space=pltpu.SMEM)],
        out_specs=(vmem, vmem),
        scratch_shapes=[
            pltpu.VMEM((rows, width), BF),
            pltpu.VMEM((rows, top), jnp.int32),
            pltpu.VMEM((rows, top), F32),
            pltpu.VMEM((1, width), F32),
            pltpu.VMEM((1, talk_width), F32),
            pltpu.VMEM((2, half, 2 * ff), BF),
            pltpu.VMEM((2, ff, half), BF),
            pltpu.VMEM((half, talk_width), BF),
            pltpu.VMEM((vocabulary, talk_width), BF),
            pltpu.VMEM((NZ, rows, META + half), BF),
            pltpu.VMEM(chunk, BF),
            pltpu.VMEM(chunk, BF),
            pltpu.VMEM(chunk, BF),
            pltpu.VMEM((slots, 2 * ff), F32),
            pltpu.VMEM((CHUNKS, slots, cw), BF),
            pltpu.VMEM((CHUNKS, slots, cw), BF),
            pltpu.VMEM((CHUNKS, slots, cw), F32),
            pltpu.VMEM(chunk, BF),
            pltpu.VMEM(chunk, BF),
            pltpu.VMEM((CHUNKS, NZ, rows, cw), BF),
            pltpu.VMEM((CHUNKS, NZ, rows, cw), BF),
            pltpu.VMEM((2 * stream, slots), BF),
            pltpu.VMEM((rows, talk_width), F32),
            pltpu.VMEM((rows, talk_width), F32),
            pltpu.VMEM((rows, talk_width), F32),
            dma((13,)),
            dma((CHUNKS,)),
            dma((CHUNKS,)),
            dma((CHUNKS,)),
            dma((CHUNKS, GROUPS)),
            dma((CHUNKS,)),
            dma((CHUNKS,)),
            dma((CHUNKS,)),
            dma((CHUNKS,)),
            dma((CHUNKS,)),
            dma((CHUNKS,)),
            dma((CHUNKS,)),
            dma((CHUNKS,)),
            dma,
            dma,
        ],
        compiler_params=pltpu.CompilerParams(
            collective_id=0, has_side_effects=True, vmem_limit_bytes=60 * 1024 * 1024
        ),
        name="expert_step",
    )(
        tokens,
        routes,
        route_weight,
        moe_gain.reshape(1, width),
        expert_gate,
        expert_up,
        expert_down,
        talker_proj,
        codebook_table,
        level_gain,
        earlier_codes,
    )
    return hidden, logits[:, None, :]


def solution(mesh):
    in_specs = (
        P("expert", None),
        P("expert", None),
        P("expert", None),
        P(),
        P("expert", None, "section"),
        P("expert", None, "section"),
        P("expert", "section", None),
        P("section", None),
        P("section", None, None),
        P("section", None),
        P("expert"),
    )
    out_specs = (P("expert", "section"), P("expert", "section", None))
    return jax.shard_map(shards, mesh=mesh, in_specs=in_specs, out_specs=out_specs, check_vma=False)
```

```python
import functools

import jax
import jax.numpy as jnp
from jax import lax
from jax.experimental import pallas as pl
from jax.experimental.pallas import tpu as pltpu
from jax.sharding import PartitionSpec as P

MESH = pl.DeviceIdType.MESH
NZ, NY, NX = 8, 4, 4
CAP = 2
CHUNKS = 4
BF, F32 = jnp.bfloat16, jnp.float32


def kernel(
    tokens_hbm, routes_hbm, weight_hbm, gain_hbm, gate_hbm, up_hbm, down_hbm, proj_hbm, table_hbm, lgain_hbm, codes_hbm,
    hidden_out, level_out, tb,
    codes, tok, rts, rwt, gain, lgain, wgu, wd, wp,
    mbuf, zbuf, sel, recv, part, acc, psend, precv, own, outb, ret, zout, zin, wmix, emb, tsend, trecv,
    load_sem, m_s, m_r, z_s, z_r, p_s, p_r, f_s, f_r, q_s, q_r, r_s, r_r, u_s, u_r, t_s, t_r,
):
    plane = NY * NX
    rows, width = tok.shape
    half = width // 2
    ff = gate_hbm.shape[2]
    top = rts.shape[0]
    cw = half // CHUNKS
    slots = plane * NZ * CAP
    span = NZ * CAP
    stream = NZ * rows
    named = top * rows
    pairs_all = NZ * named
    me = lax.axis_index("expert")
    sec = lax.axis_index("section")
    x, y, z = me % NX, (me // NX) % NY, me // plane
    other = 1 - sec

    def at_plane(dy, dx):
        return z * plane + ((y + dy) % NY) * NX + (x + dx) % NX

    def at_z(dz):
        return ((z + dz) % NZ) * plane + y * NX + x

    forth = [(o, at_plane(o // NX, o % NX)) for o in range(1, plane)]
    back = [(o, at_plane(NY - o // NX, NX - o % NX)) for o in range(1, plane)]

    barrier = pltpu.get_barrier_semaphore()
    for d in range(1, NZ):
        pl.semaphore_signal(barrier, inc=1, device_id=(at_z(d), sec), device_id_type=MESH)
    for _, peer in forth:
        pl.semaphore_signal(barrier, inc=1, device_id=(peer, sec), device_id_type=MESH)
    pl.semaphore_signal(barrier, inc=1, device_id=(me, other), device_id_type=MESH)

    pairs = [
        (tokens_hbm, tok),
        (routes_hbm, rts),
        (weight_hbm, rwt),
        (gain_hbm, gain),
        (lgain_hbm, lgain),
        (gate_hbm.at[0, pl.ds(sec * half, half), :], wgu.at[0, :, 0:ff]),
        (up_hbm.at[0, pl.ds(sec * half, half), :], wgu.at[0, :, ff : 2 * ff]),
        (gate_hbm.at[0, pl.ds(other * half, half), :], wgu.at[1, :, 0:ff]),
        (up_hbm.at[0, pl.ds(other * half, half), :], wgu.at[1, :, ff : 2 * ff]),
        (down_hbm.at[0, :, pl.ds(other * half, half)], wd.at[1]),
        (down_hbm.at[0, :, pl.ds(sec * half, half)], wd.at[0]),
        (table_hbm.at[0], tb),
        (proj_hbm, wp),
        (codes_hbm, codes),
    ]
    loads = [pltpu.make_async_copy(src, dst, load_sem.at[i]) for i, (src, dst) in enumerate(pairs)]
    for load in loads:
        load.start()

    for i in range(4):
        loads[i].wait()
    tiled = jnp.concatenate([rts[...]] * top, axis=1)
    weights = jnp.concatenate([rwt[...]] * top, axis=1)
    lane = lax.broadcasted_iota(jnp.int32, (top, named), 1)
    diagonal = lane // rows == lax.broadcasted_iota(jnp.int32, (top, named), 0)
    route = jnp.sum(jnp.where(diagonal, tiled, 0), axis=0, keepdims=True)
    rank = jnp.zeros((top, named), jnp.int32)
    for step in range(1, rows):
        same = jnp.logical_and(pltpu.roll(tiled, step, 1) == route, lane % rows >= step)
        rank += same.astype(jnp.int32)
    target = route * CAP + jnp.sum(rank, axis=0, keepdims=True)
    total = jnp.sum(weights, axis=0, keepdims=True)
    mbuf[0, 0:1, :] = target.astype(F32)
    mbuf[0, 1:2, :] = jnp.sum(jnp.where(diagonal, weights, 0.0), axis=0, keepdims=True) / total
    values = tok[...].astype(F32)
    scale = lax.rsqrt(jnp.mean(values * values, axis=1, keepdims=True) + 1e-06)
    mine = tok[:, pl.ds(sec * half, half)].astype(F32)
    mine = (mine * scale * gain[:, pl.ds(sec * half, half)]).astype(BF)
    for c in range(CHUNKS):
        zbuf[c, 0] = mine[:, c * cw : (c + 1) * cw]

    pl.semaphore_wait(barrier, NZ - 1 + plane - 1 + 1)

    def m_copy(dst, device):
        return pltpu.make_async_remote_copy(
            src_ref=mbuf.at[0] if isinstance(dst, int) else mbuf.at[dst], dst_ref=mbuf.at[dst],
            send_sem=m_s, recv_sem=m_r, device_id=(device, sec), device_id_type=MESH,
        )

    def z_copy(c, src, dst, device):
        return pltpu.make_async_remote_copy(
            src_ref=zbuf.at[c, src], dst_ref=zbuf.at[c, dst],
            send_sem=z_s.at[c], recv_sem=z_r.at[c], device_id=(device, sec), device_id_type=MESH,
        )

    others = pl.ds(1, NZ - 1)
    for d in range(1, NZ):
        m_copy(d, at_z(d)).start()
    for c in range(CHUNKS):
        for d in range(1, NZ):
            z_copy(c, 0, d, at_z(d)).start()

    slot = lax.broadcasted_iota(jnp.int32, (slots, 1), 0)
    slot_o, slot_d, slot_s = slot // span, (slot // CAP) % NZ, slot % CAP
    slot_expert = z * plane + ((y + slot_o // NX) % NY) * NX + (x + slot_o % NX) % NX
    block_base = NZ * plane * CAP
    slot_target = (slot_expert * CAP + slot_s + slot_d * block_base).astype(F32)

    def plane_copy(c, src, dst, peer, o, send, get):
        return pltpu.make_async_remote_copy(
            src_ref=src.at[c, o], dst_ref=dst.at[c, o], send_sem=send, recv_sem=get,
            device_id=(peer, sec), device_id_type=MESH,
        )

    m_copy(others, me).wait_recv()
    hits = [mbuf[d, 0:1, :] + float(d * block_base) == slot_target for d in range(NZ)]
    pick = jnp.concatenate([hit.astype(F32).astype(BF) for hit in hits], axis=1)
    for c in range(CHUNKS):
        z_copy(c, others, others, me).wait_recv()
        features = jnp.concatenate([zbuf[c, d // top] for d in range(NZ * top)], axis=0)
        chosen = jnp.dot(pick, features, preferred_element_type=F32).astype(BF).reshape(plane, span, cw)
        sel[c] = chosen
        recv[c, 0] = chosen[0]
        for o, peer in forth:
            plane_copy(c, sel, recv, peer, o, p_s.at[c], p_r.at[c]).start()

    weighted = jnp.concatenate(
        [jnp.where(hit, mbuf[d, 1:2, :], 0.0) for d, hit in enumerate(hits)], axis=1
    )
    weighted_hi = weighted.astype(BF)
    weighted_lo = (weighted - weighted_hi.astype(F32)).astype(BF)
    pair = lax.broadcasted_iota(jnp.int32, (pairs_all, stream), 0)
    row_of = (pair // named) * rows + pair % rows
    fold = (row_of == lax.broadcasted_iota(jnp.int32, (pairs_all, stream), 1)).astype(F32).astype(BF)
    across = jnp.dot(weighted_hi, fold, preferred_element_type=F32).T
    wmix[0:stream] = across.astype(BF)
    across = jnp.dot(weighted_lo, fold, preferred_element_type=F32).T
    wmix[stream:] = across.astype(BF)

    vocabulary = tb.shape[0]
    column = jnp.zeros((rows, 1), jnp.int32)
    row_at = lax.broadcasted_iota(jnp.int32, (rows, 1), 0)
    loads[13].wait()
    for i in range(rows):
        column = jnp.where(row_at == i, codes[i], column)
    code_hit = (column == lax.broadcasted_iota(jnp.int32, (rows, vocabulary), 1)).astype(F32).astype(BF)
    loads[11].wait()
    emb[...] = jnp.dot(code_hit, tb[...], preferred_element_type=F32)

    def core_copy(src, dst, send, get):
        return pltpu.make_async_remote_copy(
            src_ref=src, dst_ref=dst, send_sem=send, recv_sem=get, device_id=(me, other), device_id_type=MESH
        )

    everyone = pl.ds(1, plane - 1)
    for i in range(5, 9):
        loads[i].wait()
    for c in range(CHUNKS):
        plane_copy(c, sel, recv, me, everyone, p_s.at[c], p_r.at[c]).wait_recv()
        core_copy(recv.at[c], part.at[c], f_s.at[c], f_r.at[c]).start()
        product = jnp.dot(recv[c].reshape(slots, cw), wgu[0, c * cw : (c + 1) * cw, :], preferred_element_type=F32)
        acc[...] = product if c == 0 else acc[...] + product
    for c in range(CHUNKS):
        core_copy(recv.at[c], part.at[c], f_s.at[c], f_r.at[c]).wait_recv()
        acc[...] += jnp.dot(part[c].reshape(slots, cw), wgu[1, c * cw : (c + 1) * cw, :], preferred_element_type=F32)
    gate_val = acc[:, 0:ff]
    units = (gate_val / (1.0 + jnp.exp(-gate_val)) * acc[:, ff:]).astype(BF)

    loads[9].wait()
    for c in range(CHUNKS):
        partial = jnp.dot(units, wd[1, :, c * cw : (c + 1) * cw], preferred_element_type=F32)
        psend[c] = partial.astype(BF)
        core_copy(psend.at[c], precv.at[c], q_s.at[c], q_r.at[c]).start()
    loads[10].wait()
    for c in range(CHUNKS):
        own[c] = jnp.dot(units, wd[0, :, c * cw : (c + 1) * cw], preferred_element_type=F32)
    for c in range(CHUNKS):
        core_copy(psend.at[c], precv.at[c], q_s.at[c], q_r.at[c]).wait_recv()
        finished = (own[c] + precv[c].astype(F32)).astype(BF).reshape(plane, span, cw)
        outb[c] = finished
        ret[c, 0] = finished[0]
        for o, peer in back:
            plane_copy(c, outb, ret, peer, o, r_s.at[c], r_r.at[c]).start()

    m_copy(others, me).wait_send()
    for c in range(CHUNKS):
        z_copy(c, others, others, me).wait_send()
        plane_copy(c, sel, recv, me, everyone, p_s.at[c], p_r.at[c]).wait_send()
        core_copy(recv.at[c], part.at[c], f_s.at[c], f_r.at[c]).wait_send()

    def u_copy(c, d, device):
        return pltpu.make_async_remote_copy(
            src_ref=zout.at[c, d], dst_ref=zin.at[c, d], send_sem=u_s.at[c], recv_sem=u_r.at[c],
            device_id=(device, sec), device_id_type=MESH,
        )

    for c in range(CHUNKS):
        plane_copy(c, outb, ret, me, everyone, r_s.at[c], r_r.at[c]).wait_recv()
        both = jnp.dot(wmix[...], ret[c].reshape(slots, cw), preferred_element_type=F32)
        summed = (both[0:stream] + both[stream:]).astype(BF).reshape(NZ, rows, cw)
        zout[c] = summed
        zin[c, 0] = summed[0]
        for d in range(1, NZ):
            u_copy(c, d, at_z(NZ - d)).start()

    loads[12].wait()
    loads[4].wait()
    partial_talk = None
    for c in range(CHUNKS):
        u_copy(c, others, me).wait_recv()
        mixture = functools.reduce(jnp.add, [zin[c, d].astype(F32) for d in range(NZ)])
        at = pl.multiple_of(sec * half + c * cw, cw)
        complete = (tok[:, pl.ds(at, cw)].astype(F32) + mixture).astype(BF)
        hidden_out[:, c * cw : (c + 1) * cw] = complete
        product = jnp.dot(complete, wp[c * cw : (c + 1) * cw, :], preferred_element_type=F32)
        partial_talk = product if partial_talk is None else partial_talk + product
    tsend[...] = partial_talk + jnp.where(sec == 0, emb[...], 0.0)
    talk_copy = core_copy(tsend, trecv, t_s, t_r)
    talk_copy.start()
    for c in range(CHUNKS):
        core_copy(psend.at[c], precv.at[c], q_s.at[c], q_r.at[c]).wait_send()
        plane_copy(c, outb, ret, me, everyone, r_s.at[c], r_r.at[c]).wait_send()
        u_copy(c, others, me).wait_send()
    talk_copy.wait()

    level = partial_talk + trecv[...]
    level_scale = lax.rsqrt(jnp.mean(level * level, axis=1, keepdims=True) + 1e-06)
    level_out[...] = (level * level_scale * lgain[...]).astype(BF)


def head(hidden, level_normed, table, hidden_hbm, logits_hbm, logits, sems):
    hidden_copy = pltpu.make_async_copy(hidden, hidden_hbm, sems.at[0])
    hidden_copy.start()
    scores = lax.dot_general(level_normed[...], table[...], (((1,), (1,)), ((), ())), preferred_element_type=F32)
    logits[...] = (scores / (table.shape[1] ** 0.5)).astype(BF)
    logits_copy = pltpu.make_async_copy(logits, logits_hbm, sems.at[1])
    logits_copy.start()
    hidden_copy.wait()
    logits_copy.wait()


def shards(
    tokens,
    routes,
    route_weight,
    moe_gain,
    expert_gate,
    expert_up,
    expert_down,
    talker_proj,
    codebook_table,
    level_gain,
    earlier_codes,
):
    rows, width = tokens.shape
    top = routes.shape[1]
    half, plane = width // 2, NY * NX
    ff = expert_gate.shape[2]
    vocabulary, talk_width = codebook_table.shape[1:]
    cw = half // CHUNKS
    span, stream = NZ * CAP, NZ * rows
    slots = plane * span
    chunk = (CHUNKS, plane, span, cw)
    dma = pltpu.SemaphoreType.DMA
    hbm = pl.BlockSpec(memory_space=pltpu.HBM)
    vmem = pl.BlockSpec(memory_space=pltpu.VMEM)
    operands = (
        tokens,
        routes.T,
        route_weight.T,
        moe_gain.reshape(1, width),
        expert_gate,
        expert_up,
        expert_down,
        talker_proj,
        codebook_table,
        level_gain,
        earlier_codes,
    )
    hidden, level_normed, table = pl.pallas_call(
        kernel,
        out_shape=(
            pltpu.VMEM((rows, half), BF),
            pltpu.VMEM((rows, talk_width), BF),
            pltpu.VMEM((vocabulary, talk_width), BF),
        ),
        in_specs=[hbm] * 11,
        out_specs=(vmem,) * 3,
        scratch_shapes=[
            pltpu.SMEM((rows,), jnp.int32),
            pltpu.VMEM((rows, width), BF),
            pltpu.VMEM((top, rows), jnp.int32),
            pltpu.VMEM((top, rows), F32),
            pltpu.VMEM((1, width), F32),
            pltpu.VMEM((1, talk_width), F32),
            pltpu.VMEM((2, half, 2 * ff), BF),
            pltpu.VMEM((2, ff, half), BF),
            pltpu.VMEM((half, talk_width), BF),
            pltpu.VMEM((NZ, 2, top * rows), F32),
            pltpu.VMEM((CHUNKS, NZ, rows, cw), BF),
            pltpu.VMEM(chunk, BF),
            pltpu.VMEM(chunk, BF),
            pltpu.VMEM(chunk, BF),
            pltpu.VMEM((slots, 2 * ff), F32),
            pltpu.VMEM((CHUNKS, slots, cw), BF),
            pltpu.VMEM((CHUNKS, slots, cw), BF),
            pltpu.VMEM((CHUNKS, slots, cw), F32),
            pltpu.VMEM(chunk, BF),
            pltpu.VMEM(chunk, BF),
            pltpu.VMEM((CHUNKS, NZ, rows, cw), BF),
            pltpu.VMEM((CHUNKS, NZ, rows, cw), BF),
            pltpu.VMEM((2 * stream, slots), BF),
            pltpu.VMEM((rows, talk_width), F32),
            pltpu.VMEM((rows, talk_width), F32),
            pltpu.VMEM((rows, talk_width), F32),
            dma((14,)),
            dma,
            dma,
            dma((CHUNKS,)),
            dma((CHUNKS,)),
            dma((CHUNKS,)),
            dma((CHUNKS,)),
            dma((CHUNKS,)),
            dma((CHUNKS,)),
            dma((CHUNKS,)),
            dma((CHUNKS,)),
            dma((CHUNKS,)),
            dma((CHUNKS,)),
            dma((CHUNKS,)),
            dma((CHUNKS,)),
            dma,
            dma,
        ],
        compiler_params=pltpu.CompilerParams(
            collective_id=0, has_side_effects=True, vmem_limit_bytes=36 * 1024 * 1024
        ),
        name="expert_step",
    )(*[pltpu.with_memory_space_constraint(operand, pltpu.HBM) for operand in operands])
    hidden, logits = pl.pallas_call(
        head,
        out_shape=(
            jax.ShapeDtypeStruct((rows, half), BF),
            jax.ShapeDtypeStruct((rows, vocabulary), BF),
        ),
        in_specs=[vmem] * 3,
        out_specs=(hbm, hbm),
        scratch_shapes=[pltpu.VMEM((rows, vocabulary), BF), dma((2,))],
        compiler_params=pltpu.CompilerParams(vmem_limit_bytes=16 * 1024 * 1024),
        name="head",
    )(hidden, level_normed, table)
    return hidden, logits[:, None, :]


def solution(mesh):
    in_specs = (
        P("expert", None),
        P("expert", None),
        P("expert", None),
        P(),
        P("expert", None, "section"),
        P("expert", None, "section"),
        P("expert", "section", None),
        P("section", None),
        P("section", None, None),
        P("section", None),
        P("expert"),
    )
    out_specs = (P("expert", "section"), P("expert", "section", None))
    return jax.shard_map(shards, mesh=mesh, in_specs=in_specs, out_specs=out_specs, check_vma=False)
```

```python
import functools

import jax
import jax.numpy as jnp
from jax import lax
from jax.experimental import pallas as pl
from jax.experimental.pallas import tpu as pltpu
from jax.sharding import PartitionSpec as P

MESH = pl.DeviceIdType.MESH
NZ, NY, NX = 8, 4, 4
CAP = 2
CHUNKS = 4
BF, F32 = jnp.bfloat16, jnp.float32


def kernel(
    tokens_hbm, routes_hbm, weight_hbm, gain_hbm, gate_hbm, up_hbm, down_hbm, proj_hbm, table_hbm, lgain_hbm, codes_hbm,
    hidden_out, level_out, tb,
    codes, tok, rts, rwt, gain, lgain, wgu, wd, wp,
    mbuf, zbuf, sel, recv, acc, outb, ret, zout, zin, wmix, emb, tsend, trecv,
    load_sem, m_s, m_r, z_s, z_r, p_s, p_r, e_s, w_s, w_r, r_s, r_r, g_s, u_s, u_r, t_s, t_r,
):
    plane = NY * NX
    rows, width = tok.shape
    half = width // 2
    ff = gate_hbm.shape[2]
    top = rts.shape[0]
    cw = half // CHUNKS
    slots = plane * NZ * CAP
    span = NZ * CAP
    stream = NZ * rows
    named = top * rows
    pairs_all = NZ * named
    me = lax.axis_index("expert")
    sec = lax.axis_index("section")
    x, y, z = me % NX, (me // NX) % NY, me // plane
    other = 1 - sec

    def at_plane(dy, dx):
        return z * plane + ((y + dy) % NY) * NX + (x + dx) % NX

    def at_z(dz):
        return ((z + dz) % NZ) * plane + y * NX + x

    def apart(step, count):
        return min(step, count - step)

    offsets = sorted(range(1, plane), key=lambda o: -apart(o // NX, NY) - apart(o % NX, NX))
    forth = [(o, at_plane(o // NX, o % NX)) for o in offsets]
    z_steps = sorted(range(1, NZ), key=lambda d: -apart(d, NZ))

    hidden_columns = pl.ds(sec * ff, ff)
    up_columns = pl.ds(2 * ff + sec * ff, ff)
    pairs = [
        (tokens_hbm, tok),
        (routes_hbm, rts),
        (weight_hbm, rwt),
        (gain_hbm, gain),
        (lgain_hbm, lgain),
        (gate_hbm.at[0], wgu.at[:, hidden_columns]),
        (up_hbm.at[0], wgu.at[:, up_columns]),
        (down_hbm.at[0], wd.at[hidden_columns]),
        (table_hbm.at[0], tb),
        (proj_hbm, wp),
        (codes_hbm, codes),
    ]
    loads = [pltpu.make_async_copy(src, dst, load_sem.at[i]) for i, (src, dst) in enumerate(pairs)]
    for load in loads[:4]:
        load.start()

    barrier = pltpu.get_barrier_semaphore()

    def greet(device, core):
        pl.semaphore_signal(barrier, inc=1, device_id=(device, core), device_id_type=MESH)

    for d in z_steps:
        greet(at_z(d), sec)
    for o, peer in forth:
        greet(peer, o % 2)
    greet(me, other)
    for parity in range(2):

        @pl.when(sec == parity)
        def _():
            for o, peer in forth:
                if o % 2 == parity:
                    greet(peer, 1 - parity)

    for load in loads[4:]:
        load.start()

    for i in range(4):
        loads[i].wait()
    tiled = jnp.concatenate([rts[...]] * top, axis=1)
    weights = jnp.concatenate([rwt[...]] * top, axis=1)
    lane = lax.broadcasted_iota(jnp.int32, (top, named), 1)
    diagonal = lane // rows == lax.broadcasted_iota(jnp.int32, (top, named), 0)
    route = jnp.sum(jnp.where(diagonal, tiled, 0), axis=0, keepdims=True)
    rank = jnp.zeros((top, named), jnp.int32)
    for step in range(1, rows):
        same = jnp.logical_and(pltpu.roll(tiled, step, 1) == route, lane % rows >= step)
        rank += same.astype(jnp.int32)
    target = route * CAP + jnp.sum(rank, axis=0, keepdims=True)
    total = jnp.sum(weights, axis=0, keepdims=True)
    mbuf[0, 0:1, :] = target.astype(F32)
    mbuf[0, 1:2, :] = jnp.sum(jnp.where(diagonal, weights, 0.0), axis=0, keepdims=True) / total
    values = tok[...].astype(F32)
    scale = lax.rsqrt(jnp.mean(values * values, axis=1, keepdims=True) + 1e-06)
    mine = tok[:, pl.ds(sec * half, half)].astype(F32)
    mine = (mine * scale * gain[:, pl.ds(sec * half, half)]).astype(BF)
    for c in range(CHUNKS):
        zbuf[c, 0] = mine[:, c * cw : (c + 1) * cw]

    pl.semaphore_wait(barrier, NZ - 1 + plane - 1 + 1 + plane // 2 - 1 + sec)

    def m_copy(dst, device):
        return pltpu.make_async_remote_copy(
            src_ref=mbuf.at[0] if isinstance(dst, int) else mbuf.at[dst], dst_ref=mbuf.at[dst],
            send_sem=m_s, recv_sem=m_r, device_id=(device, sec), device_id_type=MESH,
        )

    def z_copy(c, src, dst, device):
        return pltpu.make_async_remote_copy(
            src_ref=zbuf.at[c, src], dst_ref=zbuf.at[c, dst],
            send_sem=z_s.at[c], recv_sem=z_r.at[c], device_id=(device, sec), device_id_type=MESH,
        )

    others = pl.ds(1, NZ - 1)
    for d in z_steps:
        m_copy(d, at_z(d)).start()
    for c in range(CHUNKS):
        for d in z_steps:
            z_copy(c, 0, d, at_z(d)).start()

    def core_copy(src, dst, send, get):
        return pltpu.make_async_remote_copy(
            src_ref=src, dst_ref=dst, send_sem=send, recv_sem=get, device_id=(me, other), device_id_type=MESH
        )

    shared = [core_copy(src, dst, w_s.at[i], w_r.at[i]) for i, (src, dst) in enumerate(pairs[5:8])]
    for copy in shared:
        copy.start()

    slot = lax.broadcasted_iota(jnp.int32, (slots, 1), 0)
    slot_o, slot_d, slot_s = slot // span, (slot // CAP) % NZ, slot % CAP
    slot_expert = z * plane + ((y + slot_o // NX) % NY) * NX + (x + slot_o % NX) % NX
    block_base = NZ * plane * CAP
    slot_target = (slot_expert * CAP + slot_s + slot_d * block_base).astype(F32)

    def plane_copy(src, dst, device, core, send, get):
        return pltpu.make_async_remote_copy(
            src_ref=src, dst_ref=dst, send_sem=send, recv_sem=get, device_id=(device, core), device_id_type=MESH
        )

    m_copy(others, me).wait_recv()
    hits = [mbuf[d, 0:1, :] + float(d * block_base) == slot_target for d in range(NZ)]
    pick = jnp.concatenate([hit.astype(F32).astype(BF) for hit in hits], axis=1)
    for c in range(CHUNKS):
        z_copy(c, others, others, me).wait_recv()
        features = jnp.concatenate([zbuf[c, d // top] for d in range(NZ * top)], axis=0)
        chosen = jnp.dot(pick, features, preferred_element_type=F32).astype(BF).reshape(plane, span, cw)
        sel[c] = chosen
        for o, peer in forth:
            plane_copy(sel.at[c, o], recv.at[c, sec, o // 2], peer, o % 2, p_s.at[c], p_r.at[c]).start()

        @pl.when(sec == 0)
        def _():
            pltpu.make_async_copy(sel.at[c, 0], recv.at[c, 0, 0], p_r.at[c]).start()

        @pl.when(sec == 1)
        def _():
            plane_copy(sel.at[c, 0], recv.at[c, 1, 0], me, 0, e_s.at[c], p_r.at[c]).start()

    weighted = jnp.concatenate(
        [jnp.where(hit, mbuf[d, 1:2, :], 0.0) for d, hit in enumerate(hits)], axis=1
    )
    weighted_hi = weighted.astype(BF)
    weighted_lo = (weighted - weighted_hi.astype(F32)).astype(BF)
    pair = lax.broadcasted_iota(jnp.int32, (pairs_all, stream), 0)
    row_of = (pair // named) * rows + pair % rows
    fold = (row_of == lax.broadcasted_iota(jnp.int32, (pairs_all, stream), 1)).astype(F32).astype(BF)
    across = jnp.dot(weighted_hi, fold, preferred_element_type=F32).T
    wmix[0:stream] = across.astype(BF)
    across = jnp.dot(weighted_lo, fold, preferred_element_type=F32).T
    wmix[stream:] = across.astype(BF)

    vocabulary = tb.shape[0]
    column = jnp.zeros((rows, 1), jnp.int32)
    row_at = lax.broadcasted_iota(jnp.int32, (rows, 1), 0)
    loads[10].wait()
    for i in range(rows):
        column = jnp.where(row_at == i, codes[i], column)
    code_hit = (column == lax.broadcasted_iota(jnp.int32, (rows, vocabulary), 1)).astype(F32).astype(BF)
    loads[8].wait()
    emb[...] = jnp.dot(code_hit, tb[...], preferred_element_type=F32)

    for i in range(5, 8):
        loads[i].wait()
        shared[i - 5].wait_recv()
    count = plane // 2
    held = count * span
    for c in range(CHUNKS):
        plane_copy(recv.at[c], recv.at[c], me, other, p_s.at[c], p_r.at[c]).wait_recv()
        for h in range(2):
            at = h * half + c * cw
            product = jnp.dot(recv[c, h].reshape(held, cw), wgu[at : at + cw, :], preferred_element_type=F32)
            acc[...] = product if c + h == 0 else acc[...] + product
    gate_val = acc[:, 0 : 2 * ff]
    units = (gate_val / (1.0 + jnp.exp(-gate_val)) * acc[:, 2 * ff :]).astype(BF)

    def offset_of(i):
        return 2 * i + sec

    def back_at(i):
        return at_plane(NY - i // (NX // 2), NX - 2 * (i % (NX // 2)) - sec)

    back = [(i, offset_of(i), back_at(i)) for i in range(1, count)]
    back.sort(key=lambda entry: -2 * apart(entry[0] // (NX // 2), NY) - entry[0] % (NX // 2))
    odd_home = back_at(0)
    for c in range(CHUNKS):
        for h in range(2):
            at = h * half + c * cw
            finished = jnp.dot(units, wd[:, at : at + cw], preferred_element_type=F32)
            outb[c, h] = finished.astype(BF).reshape(count, span, cw)
            for i, o, peer in back:
                plane_copy(outb.at[c, h, i], ret.at[c, o], peer, h, r_s.at[c], r_r.at[c]).start()

        @pl.when(sec == 0)
        def _():
            pltpu.make_async_copy(outb.at[c, 0, 0], ret.at[c, 0], r_r.at[c]).start()
            plane_copy(outb.at[c, 1, 0], ret.at[c, 0], me, 1, g_s.at[c], r_r.at[c]).start()

        @pl.when(sec == 1)
        def _():
            for h in range(2):
                plane_copy(outb.at[c, h, 0], ret.at[c, 1], odd_home, h, g_s.at[c], r_r.at[c]).start()

    m_copy(others, me).wait_send()
    for c in range(CHUNKS):
        z_copy(c, others, others, me).wait_send()
        sent = sel.at[c, pl.ds(1, plane - 1)]
        plane_copy(sent, sent, me, other, p_s.at[c], p_r.at[c]).wait_send()

        @pl.when(sec == 1)
        def _():
            plane_copy(sel.at[c, 0], recv.at[c, 1, 0], me, 0, e_s.at[c], p_r.at[c]).wait_send()

    for copy in shared:
        copy.wait_send()

    def u_copy(c, d, device):
        return pltpu.make_async_remote_copy(
            src_ref=zout.at[c, d], dst_ref=zin.at[c, d], send_sem=u_s.at[c], recv_sem=u_r.at[c],
            device_id=(device, sec), device_id_type=MESH,
        )

    for c in range(CHUNKS):
        plane_copy(ret.at[c], ret.at[c], me, other, r_s.at[c], r_r.at[c]).wait_recv()
        both = jnp.dot(wmix[...], ret[c].reshape(slots, cw), preferred_element_type=F32)
        summed = (both[0:stream] + both[stream:]).astype(BF).reshape(NZ, rows, cw)
        zout[c] = summed
        zin[c, 0] = summed[0]
        for d in z_steps:
            u_copy(c, d, at_z(NZ - d)).start()

    loads[9].wait()
    loads[4].wait()
    partial_talk = None
    for c in range(CHUNKS):
        u_copy(c, others, me).wait_recv()
        mixture = functools.reduce(jnp.add, [zin[c, d].astype(F32) for d in range(NZ)])
        at = pl.multiple_of(sec * half + c * cw, cw)
        complete = (tok[:, pl.ds(at, cw)].astype(F32) + mixture).astype(BF)
        hidden_out[:, c * cw : (c + 1) * cw] = complete
        product = jnp.dot(complete, wp[c * cw : (c + 1) * cw, :], preferred_element_type=F32)
        partial_talk = product if partial_talk is None else partial_talk + product
    tsend[...] = partial_talk + jnp.where(sec == 0, emb[...], 0.0)
    talk_copy = core_copy(tsend, trecv, t_s, t_r)
    talk_copy.start()
    for c in range(CHUNKS):
        sent = outb.at[c, :, pl.ds(1, count - 1)]
        plane_copy(sent, sent, me, other, r_s.at[c], r_r.at[c]).wait_send()

        @pl.when(sec == 0)
        def _():
            plane_copy(outb.at[c, 1, 0], ret.at[c, 0], me, 1, g_s.at[c], r_r.at[c]).wait_send()

        @pl.when(sec == 1)
        def _():
            sent = outb.at[c, :, 0]
            plane_copy(sent, sent, me, other, g_s.at[c], r_r.at[c]).wait_send()

        u_copy(c, others, me).wait_send()
    talk_copy.wait()

    level = partial_talk + trecv[...]
    level_scale = lax.rsqrt(jnp.mean(level * level, axis=1, keepdims=True) + 1e-06)
    level_out[...] = (level * level_scale * lgain[...]).astype(BF)


def head(hidden, level_normed, table, hidden_hbm, logits_hbm, logits, sems):
    hidden_copy = pltpu.make_async_copy(hidden, hidden_hbm, sems.at[0])
    hidden_copy.start()
    scores = lax.dot_general(level_normed[...], table[...], (((1,), (1,)), ((), ())), preferred_element_type=F32)
    logits[...] = (scores / (table.shape[1] ** 0.5)).astype(BF)
    logits_copy = pltpu.make_async_copy(logits, logits_hbm, sems.at[1])
    logits_copy.start()
    hidden_copy.wait()
    logits_copy.wait()


def shards(
    tokens,
    routes,
    route_weight,
    moe_gain,
    expert_gate,
    expert_up,
    expert_down,
    talker_proj,
    codebook_table,
    level_gain,
    earlier_codes,
):
    rows, width = tokens.shape
    top = routes.shape[1]
    half, plane = width // 2, NY * NX
    ff = expert_gate.shape[2]
    vocabulary, talk_width = codebook_table.shape[1:]
    cw = half // CHUNKS
    span, stream = NZ * CAP, NZ * rows
    slots = plane * span
    chunk = (CHUNKS, plane, span, cw)
    by_core = (CHUNKS, 2, plane // 2, span, cw)
    dma = pltpu.SemaphoreType.DMA
    hbm = pl.BlockSpec(memory_space=pltpu.HBM)
    vmem = pl.BlockSpec(memory_space=pltpu.VMEM)
    operands = (
        tokens,
        routes.T,
        route_weight.T,
        moe_gain.reshape(1, width),
        expert_gate,
        expert_up,
        expert_down,
        talker_proj,
        codebook_table,
        level_gain,
        earlier_codes,
    )
    hidden, level_normed, table = pl.pallas_call(
        kernel,
        out_shape=(
            pltpu.VMEM((rows, half), BF),
            pltpu.VMEM((rows, talk_width), BF),
            pltpu.VMEM((vocabulary, talk_width), BF),
        ),
        in_specs=[hbm] * 11,
        out_specs=(vmem,) * 3,
        scratch_shapes=[
            pltpu.SMEM((rows,), jnp.int32),
            pltpu.VMEM((rows, width), BF),
            pltpu.VMEM((top, rows), jnp.int32),
            pltpu.VMEM((top, rows), F32),
            pltpu.VMEM((1, width), F32),
            pltpu.VMEM((1, talk_width), F32),
            pltpu.VMEM((width, 4 * ff), BF),
            pltpu.VMEM((2 * ff, width), BF),
            pltpu.VMEM((half, talk_width), BF),
            pltpu.VMEM((NZ, 2, top * rows), F32),
            pltpu.VMEM((CHUNKS, NZ, rows, cw), BF),
            pltpu.VMEM(chunk, BF),
            pltpu.VMEM(by_core, BF),
            pltpu.VMEM((slots // 2, 4 * ff), F32),
            pltpu.VMEM(by_core, BF),
            pltpu.VMEM(chunk, BF),
            pltpu.VMEM((CHUNKS, NZ, rows, cw), BF),
            pltpu.VMEM((CHUNKS, NZ, rows, cw), BF),
            pltpu.VMEM((2 * stream, slots), BF),
            pltpu.VMEM((rows, talk_width), F32),
            pltpu.VMEM((rows, talk_width), F32),
            pltpu.VMEM((rows, talk_width), F32),
            dma((11,)),
            dma,
            dma,
            dma((CHUNKS,)),
            dma((CHUNKS,)),
            dma((CHUNKS,)),
            dma((CHUNKS,)),
            dma((CHUNKS,)),
            dma((3,)),
            dma((3,)),
            dma((CHUNKS,)),
            dma((CHUNKS,)),
            dma((CHUNKS,)),
            dma((CHUNKS,)),
            dma((CHUNKS,)),
            dma,
            dma,
        ],
        compiler_params=pltpu.CompilerParams(
            collective_id=0, has_side_effects=True, vmem_limit_bytes=40 * 1024 * 1024
        ),
        name="expert_step",
    )(*[pltpu.with_memory_space_constraint(operand, pltpu.HBM) for operand in operands])
    hidden, logits = pl.pallas_call(
        head,
        out_shape=(
            jax.ShapeDtypeStruct((rows, half), BF),
            jax.ShapeDtypeStruct((rows, vocabulary), BF),
        ),
        in_specs=[vmem] * 3,
        out_specs=(hbm, hbm),
        scratch_shapes=[pltpu.VMEM((rows, vocabulary), BF), dma((2,))],
        compiler_params=pltpu.CompilerParams(vmem_limit_bytes=16 * 1024 * 1024),
        name="head",
    )(hidden, level_normed, table)
    return hidden, logits[:, None, :]


def solution(mesh):
    in_specs = (
        P("expert", None),
        P("expert", None),
        P("expert", None),
        P(),
        P("expert", None, "section"),
        P("expert", None, "section"),
        P("expert", "section", None),
        P("section", None),
        P("section", None, None),
        P("section", None),
        P("expert"),
    )
    out_specs = (P("expert", "section"), P("expert", "section", None))
    return jax.shard_map(shards, mesh=mesh, in_specs=in_specs, out_specs=out_specs, check_vma=False)
```

```python
import functools

import jax
import jax.numpy as jnp
from jax import lax
from jax.experimental import pallas as pl
from jax.experimental.pallas import tpu as pltpu
from jax.sharding import PartitionSpec as P

MESH = pl.DeviceIdType.MESH
NZ, NY, NX = 8, 4, 4
CAP = 2
CHUNKS = 4
BF, F32 = jnp.bfloat16, jnp.float32


def kernel(
    tokens_hbm, routes_hbm, weight_hbm, gain_hbm, gate_hbm, up_hbm, down_hbm, proj_hbm, table_hbm, lgain_hbm, codes_hbm,
    hidden_out, level_out, across_out,
    tb, codes, tok, rts, rwt, gain, lgain, wgu, wd, wp,
    mbuf, zbuf, sel, recv, acc, outb, ret, zout, zin, wmix, emb, tsend, trecv,
    load_sem, m_s, m_r, z_s, z_r, p_s, p_r, e_s, w_s, w_r, r_s, r_r, g_s, u_s, u_r, t_s, t_r,
):
    plane = NY * NX
    rows, width = tok.shape
    half = width // 2
    ff = gate_hbm.shape[2]
    top = rts.shape[0]
    cw = half // CHUNKS
    slots = plane * NZ * CAP
    span = NZ * CAP
    stream = NZ * rows
    named = top * rows
    pairs_all = NZ * named
    me = lax.axis_index("expert")
    sec = lax.axis_index("section")
    x, y, z = me % NX, (me // NX) % NY, me // plane
    other = 1 - sec

    def at_plane(dy, dx):
        return z * plane + ((y + dy) % NY) * NX + (x + dx) % NX

    def at_z(dz):
        return ((z + dz) % NZ) * plane + y * NX + x

    def apart(step, count):
        return min(step, count - step)

    offsets = sorted(range(1, plane), key=lambda o: -apart(o // NX, NY) - apart(o % NX, NX))
    forth = [(o, at_plane(o // NX, o % NX)) for o in offsets]
    z_steps = sorted(range(1, NZ), key=lambda d: -apart(d, NZ))

    hidden_columns = pl.ds(sec * ff, ff)
    up_columns = pl.ds(2 * ff + sec * ff, ff)
    pairs = [
        (tokens_hbm, tok),
        (routes_hbm, rts),
        (weight_hbm, rwt),
        (gain_hbm, gain),
        (lgain_hbm, lgain),
        (gate_hbm.at[0], wgu.at[:, hidden_columns]),
        (up_hbm.at[0], wgu.at[:, up_columns]),
        (down_hbm.at[0], wd.at[hidden_columns]),
        (table_hbm.at[0], tb),
        (proj_hbm, wp),
        (codes_hbm, codes),
    ]
    loads = [pltpu.make_async_copy(src, dst, load_sem.at[i]) for i, (src, dst) in enumerate(pairs)]
    for load in loads[:4]:
        load.start()

    barrier = pltpu.get_barrier_semaphore()

    def greet(device, core):
        pl.semaphore_signal(barrier, inc=1, device_id=(device, core), device_id_type=MESH)

    for d in z_steps:
        greet(at_z(d), sec)
    for o, peer in forth:
        greet(peer, o % 2)
    greet(me, other)
    for parity in range(2):

        @pl.when(sec == parity)
        def _():
            for o, peer in forth:
                if o % 2 == parity:
                    greet(peer, 1 - parity)

    for load in loads[4:]:
        load.start()

    for i in range(4):
        loads[i].wait()
    tiled = jnp.concatenate([rts[...]] * top, axis=1)
    weights = jnp.concatenate([rwt[...]] * top, axis=1)
    lane = lax.broadcasted_iota(jnp.int32, (top, named), 1)
    diagonal = lane // rows == lax.broadcasted_iota(jnp.int32, (top, named), 0)
    route = jnp.sum(jnp.where(diagonal, tiled, 0), axis=0, keepdims=True)
    rank = jnp.zeros((top, named), jnp.int32)
    for step in range(1, rows):
        same = jnp.logical_and(pltpu.roll(tiled, step, 1) == route, lane % rows >= step)
        rank += same.astype(jnp.int32)
    target = route * CAP + jnp.sum(rank, axis=0, keepdims=True)
    total = jnp.sum(weights, axis=0, keepdims=True)
    mbuf[0, 0:1, :] = target.astype(F32)
    mbuf[0, 1:2, :] = jnp.sum(jnp.where(diagonal, weights, 0.0), axis=0, keepdims=True) / total
    values = tok[...].astype(F32)
    scale = lax.rsqrt(jnp.mean(values * values, axis=1, keepdims=True) + 1e-06)
    mine = tok[:, pl.ds(sec * half, half)].astype(F32)
    mine = (mine * scale * gain[:, pl.ds(sec * half, half)]).astype(BF)
    for c in range(CHUNKS):
        zbuf[c, 0] = mine[:, c * cw : (c + 1) * cw]

    pl.semaphore_wait(barrier, NZ - 1 + plane - 1 + 1 + plane // 2 - 1 + sec)

    def m_copy(dst, device):
        return pltpu.make_async_remote_copy(
            src_ref=mbuf.at[0] if isinstance(dst, int) else mbuf.at[dst], dst_ref=mbuf.at[dst],
            send_sem=m_s, recv_sem=m_r, device_id=(device, sec), device_id_type=MESH,
        )

    def z_copy(c, src, dst, device):
        return pltpu.make_async_remote_copy(
            src_ref=zbuf.at[c, src], dst_ref=zbuf.at[c, dst],
            send_sem=z_s.at[c], recv_sem=z_r.at[c], device_id=(device, sec), device_id_type=MESH,
        )

    others = pl.ds(1, NZ - 1)
    for d in z_steps:
        m_copy(d, at_z(d)).start()
    for c in range(CHUNKS):
        for d in z_steps:
            z_copy(c, 0, d, at_z(d)).start()

    def core_copy(src, dst, send, get):
        return pltpu.make_async_remote_copy(
            src_ref=src, dst_ref=dst, send_sem=send, recv_sem=get, device_id=(me, other), device_id_type=MESH
        )

    shared = [core_copy(src, dst, w_s.at[i], w_r.at[i]) for i, (src, dst) in enumerate(pairs[5:8])]
    for copy in shared:
        copy.start()

    slot = lax.broadcasted_iota(jnp.int32, (slots, 1), 0)
    slot_o, slot_d, slot_s = slot // span, (slot // CAP) % NZ, slot % CAP
    slot_expert = z * plane + ((y + slot_o // NX) % NY) * NX + (x + slot_o % NX) % NX
    block_base = NZ * plane * CAP
    slot_target = (slot_expert * CAP + slot_s + slot_d * block_base).astype(F32)

    def plane_copy(src, dst, device, core, send, get):
        return pltpu.make_async_remote_copy(
            src_ref=src, dst_ref=dst, send_sem=send, recv_sem=get, device_id=(device, core), device_id_type=MESH
        )

    m_copy(others, me).wait_recv()
    hits = [mbuf[d, 0:1, :] + float(d * block_base) == slot_target for d in range(NZ)]
    pick = jnp.concatenate([hit.astype(F32).astype(BF) for hit in hits], axis=1)
    for c in range(CHUNKS):
        z_copy(c, others, others, me).wait_recv()
        features = jnp.concatenate([zbuf[c, d // top] for d in range(NZ * top)], axis=0)
        chosen = jnp.dot(pick, features, preferred_element_type=F32).astype(BF).reshape(plane, span, cw)
        sel[c] = chosen
        for o, peer in forth:
            plane_copy(sel.at[c, o], recv.at[c, sec, o // 2], peer, o % 2, p_s.at[c], p_r.at[c]).start()

        @pl.when(sec == 0)
        def _():
            pltpu.make_async_copy(sel.at[c, 0], recv.at[c, 0, 0], p_r.at[c]).start()

        @pl.when(sec == 1)
        def _():
            plane_copy(sel.at[c, 0], recv.at[c, 1, 0], me, 0, e_s.at[c], p_r.at[c]).start()

    weighted = jnp.concatenate(
        [jnp.where(hit, mbuf[d, 1:2, :], 0.0) for d, hit in enumerate(hits)], axis=1
    )
    weighted_hi = weighted.astype(BF)
    weighted_lo = (weighted - weighted_hi.astype(F32)).astype(BF)
    pair = lax.broadcasted_iota(jnp.int32, (pairs_all, stream), 0)
    row_of = (pair // named) * rows + pair % rows
    fold = (row_of == lax.broadcasted_iota(jnp.int32, (pairs_all, stream), 1)).astype(F32).astype(BF)
    across = jnp.dot(weighted_hi, fold, preferred_element_type=F32).T
    wmix[0:stream] = across.astype(BF)
    across = jnp.dot(weighted_lo, fold, preferred_element_type=F32).T
    wmix[stream:] = across.astype(BF)

    vocabulary = tb.shape[0]
    column = jnp.zeros((rows, 1), jnp.int32)
    row_at = lax.broadcasted_iota(jnp.int32, (rows, 1), 0)
    loads[10].wait()
    for i in range(rows):
        column = jnp.where(row_at == i, codes[i], column)
    code_hit = (column == lax.broadcasted_iota(jnp.int32, (rows, vocabulary), 1)).astype(F32).astype(BF)
    loads[8].wait()
    emb[...] = jnp.dot(code_hit, tb[...], preferred_element_type=F32)

    strip = vocabulary // 8
    for i in range(8):
        across_out[:, i * strip : (i + 1) * strip] = tb[i * strip : (i + 1) * strip, :].T

    for i in range(5, 8):
        loads[i].wait()
        shared[i - 5].wait_recv()
    count = plane // 2
    held = count * span
    for c in range(CHUNKS):
        plane_copy(recv.at[c], recv.at[c], me, other, p_s.at[c], p_r.at[c]).wait_recv()
        for h in range(2):
            at = h * half + c * cw
            product = jnp.dot(recv[c, h].reshape(held, cw), wgu[at : at + cw, :], preferred_element_type=F32)
            acc[...] = product if c + h == 0 else acc[...] + product
    gate_val = acc[:, 0 : 2 * ff]
    units = (gate_val / (1.0 + jnp.exp(-gate_val)) * acc[:, 2 * ff :]).astype(BF)

    def offset_of(i):
        return 2 * i + sec

    def back_at(i):
        return at_plane(NY - i // (NX // 2), NX - 2 * (i % (NX // 2)) - sec)

    back = [(i, offset_of(i), back_at(i)) for i in range(1, count)]
    back.sort(key=lambda entry: -2 * apart(entry[0] // (NX // 2), NY) - entry[0] % (NX // 2))
    odd_home = back_at(0)
    for c in range(CHUNKS):
        for h in range(2):
            at = h * half + c * cw
            finished = jnp.dot(units, wd[:, at : at + cw], preferred_element_type=F32)
            outb[c, h] = finished.astype(BF).reshape(count, span, cw)
            for i, o, peer in back:
                plane_copy(outb.at[c, h, i], ret.at[c, o], peer, h, r_s.at[c], r_r.at[c]).start()

        @pl.when(sec == 0)
        def _():
            pltpu.make_async_copy(outb.at[c, 0, 0], ret.at[c, 0], r_r.at[c]).start()
            plane_copy(outb.at[c, 1, 0], ret.at[c, 0], me, 1, g_s.at[c], r_r.at[c]).start()

        @pl.when(sec == 1)
        def _():
            for h in range(2):
                plane_copy(outb.at[c, h, 0], ret.at[c, 1], odd_home, h, g_s.at[c], r_r.at[c]).start()

    m_copy(others, me).wait_send()
    for c in range(CHUNKS):
        z_copy(c, others, others, me).wait_send()
        sent = sel.at[c, pl.ds(1, plane - 1)]
        plane_copy(sent, sent, me, other, p_s.at[c], p_r.at[c]).wait_send()

        @pl.when(sec == 1)
        def _():
            plane_copy(sel.at[c, 0], recv.at[c, 1, 0], me, 0, e_s.at[c], p_r.at[c]).wait_send()

    for copy in shared:
        copy.wait_send()

    def u_copy(c, d, device):
        return pltpu.make_async_remote_copy(
            src_ref=zout.at[c, d], dst_ref=zin.at[c, d], send_sem=u_s.at[c], recv_sem=u_r.at[c],
            device_id=(device, sec), device_id_type=MESH,
        )

    for c in range(CHUNKS):
        plane_copy(ret.at[c], ret.at[c], me, other, r_s.at[c], r_r.at[c]).wait_recv()
        both = jnp.dot(wmix[...], ret[c].reshape(slots, cw), preferred_element_type=F32)
        summed = (both[0:stream] + both[stream:]).astype(BF).reshape(NZ, rows, cw)
        zout[c] = summed
        zin[c, 0] = summed[0]
        for d in z_steps:
            u_copy(c, d, at_z(NZ - d)).start()

    loads[9].wait()
    loads[4].wait()
    partial_talk = None
    for c in range(CHUNKS):
        u_copy(c, others, me).wait_recv()
        mixture = functools.reduce(jnp.add, [zin[c, d].astype(F32) for d in range(NZ)])
        at = pl.multiple_of(sec * half + c * cw, cw)
        complete = (tok[:, pl.ds(at, cw)].astype(F32) + mixture).astype(BF)
        hidden_out[:, c * cw : (c + 1) * cw] = complete
        product = jnp.dot(complete, wp[c * cw : (c + 1) * cw, :], preferred_element_type=F32)
        partial_talk = product if partial_talk is None else partial_talk + product
    tsend[...] = partial_talk + jnp.where(sec == 0, emb[...], 0.0)
    talk_copy = core_copy(tsend, trecv, t_s, t_r)
    talk_copy.start()
    for c in range(CHUNKS):
        sent = outb.at[c, :, pl.ds(1, count - 1)]
        plane_copy(sent, sent, me, other, r_s.at[c], r_r.at[c]).wait_send()

        @pl.when(sec == 0)
        def _():
            plane_copy(outb.at[c, 1, 0], ret.at[c, 0], me, 1, g_s.at[c], r_r.at[c]).wait_send()

        @pl.when(sec == 1)
        def _():
            sent = outb.at[c, :, 0]
            plane_copy(sent, sent, me, other, g_s.at[c], r_r.at[c]).wait_send()

        u_copy(c, others, me).wait_send()
    talk_copy.wait()

    level = partial_talk + trecv[...]
    level_scale = lax.rsqrt(jnp.mean(level * level, axis=1, keepdims=True) + 1e-06)
    level_out[...] = (level * level_scale * lgain[...]).astype(BF)


def head(hidden, level_normed, table, hidden_hbm, logits_hbm, logits, sems):
    hidden_copy = pltpu.make_async_copy(hidden, hidden_hbm, sems.at[0])
    hidden_copy.start()
    scores = jnp.dot(level_normed[...], table[...], preferred_element_type=F32)
    logits[...] = (scores / (table.shape[0] ** 0.5)).astype(BF)
    logits_copy = pltpu.make_async_copy(logits, logits_hbm, sems.at[1])
    logits_copy.start()
    hidden_copy.wait()
    logits_copy.wait()


def shards(
    tokens,
    routes,
    route_weight,
    moe_gain,
    expert_gate,
    expert_up,
    expert_down,
    talker_proj,
    codebook_table,
    level_gain,
    earlier_codes,
):
    rows, width = tokens.shape
    top = routes.shape[1]
    half, plane = width // 2, NY * NX
    ff = expert_gate.shape[2]
    vocabulary, talk_width = codebook_table.shape[1:]
    cw = half // CHUNKS
    span, stream = NZ * CAP, NZ * rows
    slots = plane * span
    chunk = (CHUNKS, plane, span, cw)
    by_core = (CHUNKS, 2, plane // 2, span, cw)
    dma = pltpu.SemaphoreType.DMA
    hbm = pl.BlockSpec(memory_space=pltpu.HBM)
    vmem = pl.BlockSpec(memory_space=pltpu.VMEM)
    operands = (
        tokens,
        routes.T,
        route_weight.T,
        moe_gain.reshape(1, width),
        expert_gate,
        expert_up,
        expert_down,
        talker_proj,
        codebook_table,
        level_gain,
        earlier_codes,
    )
    hidden, level_normed, table = pl.pallas_call(
        kernel,
        out_shape=(
            pltpu.VMEM((rows, half), BF),
            pltpu.VMEM((rows, talk_width), BF),
            pltpu.VMEM((talk_width, vocabulary), BF),
        ),
        in_specs=[hbm] * 11,
        out_specs=(vmem,) * 3,
        scratch_shapes=[
            pltpu.VMEM((vocabulary, talk_width), BF),
            pltpu.SMEM((rows,), jnp.int32),
            pltpu.VMEM((rows, width), BF),
            pltpu.VMEM((top, rows), jnp.int32),
            pltpu.VMEM((top, rows), F32),
            pltpu.VMEM((1, width), F32),
            pltpu.VMEM((1, talk_width), F32),
            pltpu.VMEM((width, 4 * ff), BF),
            pltpu.VMEM((2 * ff, width), BF),
            pltpu.VMEM((half, talk_width), BF),
            pltpu.VMEM((NZ, 2, top * rows), F32),
            pltpu.VMEM((CHUNKS, NZ, rows, cw), BF),
            pltpu.VMEM(chunk, BF),
            pltpu.VMEM(by_core, BF),
            pltpu.VMEM((slots // 2, 4 * ff), F32),
            pltpu.VMEM(by_core, BF),
            pltpu.VMEM(chunk, BF),
            pltpu.VMEM((CHUNKS, NZ, rows, cw), BF),
            pltpu.VMEM((CHUNKS, NZ, rows, cw), BF),
            pltpu.VMEM((2 * stream, slots), BF),
            pltpu.VMEM((rows, talk_width), F32),
            pltpu.VMEM((rows, talk_width), F32),
            pltpu.VMEM((rows, talk_width), F32),
            dma((11,)),
            dma,
            dma,
            dma((CHUNKS,)),
            dma((CHUNKS,)),
            dma((CHUNKS,)),
            dma((CHUNKS,)),
            dma((CHUNKS,)),
            dma((3,)),
            dma((3,)),
            dma((CHUNKS,)),
            dma((CHUNKS,)),
            dma((CHUNKS,)),
            dma((CHUNKS,)),
            dma((CHUNKS,)),
            dma,
            dma,
        ],
        compiler_params=pltpu.CompilerParams(
            collective_id=0, has_side_effects=True, vmem_limit_bytes=44 * 1024 * 1024
        ),
        name="expert_step",
    )(*[pltpu.with_memory_space_constraint(operand, pltpu.HBM) for operand in operands])
    hidden, logits = pl.pallas_call(
        head,
        out_shape=(
            jax.ShapeDtypeStruct((rows, half), BF),
            jax.ShapeDtypeStruct((rows, vocabulary), BF),
        ),
        in_specs=[vmem] * 3,
        out_specs=(hbm, hbm),
        scratch_shapes=[pltpu.VMEM((rows, vocabulary), BF), dma((2,))],
        compiler_params=pltpu.CompilerParams(vmem_limit_bytes=16 * 1024 * 1024),
        name="head",
    )(hidden, level_normed, table)
    return hidden, logits[:, None, :]


def solution(mesh):
    in_specs = (
        P("expert", None),
        P("expert", None),
        P("expert", None),
        P(),
        P("expert", None, "section"),
        P("expert", None, "section"),
        P("expert", "section", None),
        P("section", None),
        P("section", None, None),
        P("section", None),
        P("expert"),
    )
    out_specs = (P("expert", "section"), P("expert", "section", None))
    return jax.shard_map(shards, mesh=mesh, in_specs=in_specs, out_specs=out_specs, check_vma=False)
```

```python
import functools

import jax
import jax.numpy as jnp
from jax import lax
from jax.experimental import pallas as pl
from jax.experimental.pallas import tpu as pltpu
from jax.sharding import PartitionSpec as P

MESH = pl.DeviceIdType.MESH
NZ, NY, NX = 8, 4, 4
CAP = 2
CHUNKS = 4
BF, F32 = jnp.bfloat16, jnp.float32


def kernel(
    tokens_hbm, routes_hbm, weight_hbm, gain_hbm, gate_hbm, up_hbm, down_hbm, proj_hbm, table_hbm, lgain_hbm, codes_hbm,
    hidden_out, level_out, across_out,
    tb, codes, tok, rts, rwt, gain, lgain, wgu, wd, wp,
    mbuf, zbuf, sel, recv, acc, outb, ret, zout, zin, wmix, emb, tsend, trecv,
    load_sem, m_s, m_r, z_s, z_r, p_s, p_r, e_s, w_s, w_r, r_s, r_r, g_s, u_s, u_r, t_s, t_r,
):
    plane = NY * NX
    rows, width = tok.shape
    half = width // 2
    ff = gate_hbm.shape[2]
    top = rts.shape[0]
    cw = half // CHUNKS
    slots = plane * NZ * CAP
    span = NZ * CAP
    stream = NZ * rows
    named = top * rows
    pairs_all = NZ * named
    me = lax.axis_index("expert")
    sec = lax.axis_index("section")
    x, y, z = me % NX, (me // NX) % NY, me // plane
    other = 1 - sec

    def at_plane(dy, dx):
        return z * plane + ((y + dy) % NY) * NX + (x + dx) % NX

    def at_z(dz):
        return ((z + dz) % NZ) * plane + y * NX + x

    def apart(step, count):
        return min(step, count - step)

    offsets = sorted(range(1, plane), key=lambda o: -apart(o // NX, NY) - apart(o % NX, NX))
    forth = [(o, at_plane(o // NX, o % NX)) for o in offsets]
    z_steps = sorted(range(1, NZ), key=lambda d: -apart(d, NZ))

    hidden_columns = pl.ds(sec * ff, ff)
    up_columns = pl.ds(2 * ff + sec * ff, ff)
    pairs = [
        (tokens_hbm, tok),
        (routes_hbm, rts),
        (weight_hbm, rwt),
        (gain_hbm, gain),
        (lgain_hbm, lgain),
        (gate_hbm.at[0], wgu.at[:, hidden_columns]),
        (up_hbm.at[0], wgu.at[:, up_columns]),
        (down_hbm.at[0], wd.at[hidden_columns]),
        (table_hbm.at[0], tb),
        (proj_hbm, wp),
        (codes_hbm, codes),
    ]
    loads = [pltpu.make_async_copy(src, dst, load_sem.at[i]) for i, (src, dst) in enumerate(pairs)]
    for load in loads[:4]:
        load.start()

    barrier = pltpu.get_barrier_semaphore()

    def greet(device, core):
        pl.semaphore_signal(barrier, inc=1, device_id=(device, core), device_id_type=MESH)

    for d in z_steps:
        greet(at_z(d), sec)
    for o, peer in forth:
        greet(peer, o % 2)
    greet(me, other)
    for parity in range(2):

        @pl.when(sec == parity)
        def _():
            for o, peer in forth:
                if o % 2 == parity:
                    greet(peer, 1 - parity)

    for load in loads[4:]:
        load.start()

    for i in range(4):
        loads[i].wait()
    tiled = jnp.concatenate([rts[...]] * top, axis=1)
    weights = jnp.concatenate([rwt[...]] * top, axis=1)
    lane = lax.broadcasted_iota(jnp.int32, (top, named), 1)
    diagonal = lane // rows == lax.broadcasted_iota(jnp.int32, (top, named), 0)
    route = jnp.sum(jnp.where(diagonal, tiled, 0), axis=0, keepdims=True)
    rank = jnp.zeros((top, named), jnp.int32)
    for step in range(1, rows):
        same = jnp.logical_and(pltpu.roll(tiled, step, 1) == route, lane % rows >= step)
        rank += same.astype(jnp.int32)
    target = route * CAP + jnp.sum(rank, axis=0, keepdims=True)
    total = jnp.sum(weights, axis=0, keepdims=True)
    mbuf[0, 0:1, :] = target.astype(F32)
    mbuf[0, 1:2, :] = jnp.sum(jnp.where(diagonal, weights, 0.0), axis=0, keepdims=True) / total
    values = tok[...].astype(F32)
    scale = lax.rsqrt(jnp.mean(values * values, axis=1, keepdims=True) + 1e-06)
    mine = tok[:, pl.ds(sec * half, half)].astype(F32)
    mine = (mine * scale * gain[:, pl.ds(sec * half, half)]).astype(BF)
    for c in range(CHUNKS):
        zbuf[c, 0] = mine[:, c * cw : (c + 1) * cw]

    pl.semaphore_wait(barrier, NZ - 1 + plane - 1 + 1 + plane // 2 - 1 + sec)

    def m_copy(dst, device):
        return pltpu.make_async_remote_copy(
            src_ref=mbuf.at[0] if isinstance(dst, int) else mbuf.at[dst], dst_ref=mbuf.at[dst],
            send_sem=m_s, recv_sem=m_r, device_id=(device, sec), device_id_type=MESH,
        )

    def z_copy(c, src, dst, device):
        return pltpu.make_async_remote_copy(
            src_ref=zbuf.at[c, src], dst_ref=zbuf.at[c, dst],
            send_sem=z_s.at[c], recv_sem=z_r.at[c], device_id=(device, sec), device_id_type=MESH,
        )

    others = pl.ds(1, NZ - 1)
    for d in z_steps:
        m_copy(d, at_z(d)).start()
    for c in range(CHUNKS):
        for d in z_steps:
            z_copy(c, 0, d, at_z(d)).start()

    def core_copy(src, dst, send, get):
        return pltpu.make_async_remote_copy(
            src_ref=src, dst_ref=dst, send_sem=send, recv_sem=get, device_id=(me, other), device_id_type=MESH
        )

    shared = [core_copy(src, dst, w_s.at[i], w_r.at[i]) for i, (src, dst) in enumerate(pairs[5:8])]
    for copy in shared:
        copy.start()

    slot = lax.broadcasted_iota(jnp.int32, (slots, 1), 0)
    slot_o, slot_d, slot_s = slot // span, (slot // CAP) % NZ, slot % CAP
    slot_expert = z * plane + ((y + slot_o // NX) % NY) * NX + (x + slot_o % NX) % NX
    block_base = NZ * plane * CAP
    slot_target = (slot_expert * CAP + slot_s + slot_d * block_base).astype(F32)

    def plane_copy(src, dst, device, core, send, get):
        return pltpu.make_async_remote_copy(
            src_ref=src, dst_ref=dst, send_sem=send, recv_sem=get, device_id=(device, core), device_id_type=MESH
        )

    m_copy(others, me).wait_recv()
    hits = [mbuf[d, 0:1, :] + float(d * block_base) == slot_target for d in range(NZ)]
    pick = jnp.concatenate([hit.astype(F32).astype(BF) for hit in hits], axis=1)
    pair = lax.broadcasted_iota(jnp.int32, (pairs_all, stream), 0)
    row_of = (pair // named) * rows + pair % rows
    fold = (row_of == lax.broadcasted_iota(jnp.int32, (pairs_all, stream), 1)).astype(F32).astype(BF)
    pick = jnp.dot(pick, fold, preferred_element_type=F32).astype(BF)
    for c in range(CHUNKS):
        z_copy(c, others, others, me).wait_recv()
        features = zbuf[c].reshape(stream, cw)
        chosen = jnp.dot(pick, features, preferred_element_type=F32).astype(BF).reshape(plane, span, cw)
        sel[c] = chosen
        for o, peer in forth:
            plane_copy(sel.at[c, o], recv.at[c, sec, o // 2], peer, o % 2, p_s.at[c], p_r.at[c]).start()

        @pl.when(sec == 0)
        def _():
            pltpu.make_async_copy(sel.at[c, 0], recv.at[c, 0, 0], p_r.at[c]).start()

        @pl.when(sec == 1)
        def _():
            plane_copy(sel.at[c, 0], recv.at[c, 1, 0], me, 0, e_s.at[c], p_r.at[c]).start()

    weighted = jnp.concatenate(
        [jnp.where(hit, mbuf[d, 1:2, :], 0.0) for d, hit in enumerate(hits)], axis=1
    )
    weighted_hi = weighted.astype(BF)
    weighted_lo = (weighted - weighted_hi.astype(F32)).astype(BF)
    across = jnp.dot(weighted_hi, fold, preferred_element_type=F32).T
    wmix[0:stream] = across.astype(BF)
    across = jnp.dot(weighted_lo, fold, preferred_element_type=F32).T
    wmix[stream:] = across.astype(BF)

    vocabulary = tb.shape[0]
    column = jnp.zeros((rows, 1), jnp.int32)
    row_at = lax.broadcasted_iota(jnp.int32, (rows, 1), 0)
    loads[10].wait()
    for i in range(rows):
        column = jnp.where(row_at == i, codes[i], column)
    code_hit = (column == lax.broadcasted_iota(jnp.int32, (rows, vocabulary), 1)).astype(F32).astype(BF)
    loads[8].wait()
    emb[...] = jnp.dot(code_hit, tb[...], preferred_element_type=F32)

    strip = vocabulary // 8
    for i in range(8):
        across_out[:, i * strip : (i + 1) * strip] = tb[i * strip : (i + 1) * strip, :].T

    for i in range(5, 8):
        loads[i].wait()
        shared[i - 5].wait_recv()
    count = plane // 2
    held = count * span
    for c in range(CHUNKS):
        plane_copy(recv.at[c], recv.at[c], me, other, p_s.at[c], p_r.at[c]).wait_recv()
        product = jnp.dot(recv[c, 0].reshape(held, cw), wgu[c * cw : (c + 1) * cw, :], preferred_element_type=F32)
        at = half + c * cw
        product += jnp.dot(recv[c, 1].reshape(held, cw), wgu[at : at + cw, :], preferred_element_type=F32)
        acc[...] = product if c == 0 else acc[...] + product
    gate_val = acc[:, 0 : 2 * ff]
    units = (gate_val / (1.0 + jnp.exp(-gate_val)) * acc[:, 2 * ff :]).astype(BF)

    def offset_of(i):
        return 2 * i + sec

    def back_at(i):
        return at_plane(NY - i // (NX // 2), NX - 2 * (i % (NX // 2)) - sec)

    back = [(i, offset_of(i), back_at(i)) for i in range(1, count)]
    back.sort(key=lambda entry: -2 * apart(entry[0] // (NX // 2), NY) - entry[0] % (NX // 2))
    odd_home = back_at(0)
    for c in range(CHUNKS):
        for h in range(2):
            at = h * half + c * cw
            finished = jnp.dot(units, wd[:, at : at + cw], preferred_element_type=F32)
            outb[c, h] = finished.astype(BF).reshape(count, span, cw)
            for i, o, peer in back:
                plane_copy(outb.at[c, h, i], ret.at[c, o], peer, h, r_s.at[c], r_r.at[c]).start()

        @pl.when(sec == 0)
        def _():
            pltpu.make_async_copy(outb.at[c, 0, 0], ret.at[c, 0], r_r.at[c]).start()
            plane_copy(outb.at[c, 1, 0], ret.at[c, 0], me, 1, g_s.at[c], r_r.at[c]).start()

        @pl.when(sec == 1)
        def _():
            for h in range(2):
                plane_copy(outb.at[c, h, 0], ret.at[c, 1], odd_home, h, g_s.at[c], r_r.at[c]).start()

    m_copy(others, me).wait_send()
    for c in range(CHUNKS):
        z_copy(c, others, others, me).wait_send()
        sent = sel.at[c, pl.ds(1, plane - 1)]
        plane_copy(sent, sent, me, other, p_s.at[c], p_r.at[c]).wait_send()

        @pl.when(sec == 1)
        def _():
            plane_copy(sel.at[c, 0], recv.at[c, 1, 0], me, 0, e_s.at[c], p_r.at[c]).wait_send()

    for copy in shared:
        copy.wait_send()

    def u_copy(c, d, device):
        return pltpu.make_async_remote_copy(
            src_ref=zout.at[c, d], dst_ref=zin.at[c, d], send_sem=u_s.at[c], recv_sem=u_r.at[c],
            device_id=(device, sec), device_id_type=MESH,
        )

    for c in range(CHUNKS):
        plane_copy(ret.at[c], ret.at[c], me, other, r_s.at[c], r_r.at[c]).wait_recv()
        both = jnp.dot(wmix[...], ret[c].reshape(slots, cw), preferred_element_type=F32)
        summed = (both[0:stream] + both[stream:]).astype(BF).reshape(NZ, rows, cw)
        zout[c] = summed
        zin[c, 0] = summed[0]
        for d in z_steps:
            u_copy(c, d, at_z(NZ - d)).start()

    loads[9].wait()
    loads[4].wait()
    partial_talk = None
    for c in range(CHUNKS):
        u_copy(c, others, me).wait_recv()
        mixture = functools.reduce(jnp.add, [zin[c, d].astype(F32) for d in range(NZ)])
        at = pl.multiple_of(sec * half + c * cw, cw)
        complete = (tok[:, pl.ds(at, cw)].astype(F32) + mixture).astype(BF)
        hidden_out[:, c * cw : (c + 1) * cw] = complete
        product = jnp.dot(complete, wp[c * cw : (c + 1) * cw, :], preferred_element_type=F32)
        partial_talk = product if partial_talk is None else partial_talk + product
    tsend[...] = partial_talk + jnp.where(sec == 0, emb[...], 0.0)
    talk_copy = core_copy(tsend, trecv, t_s, t_r)
    talk_copy.start()
    for c in range(CHUNKS):
        sent = outb.at[c, :, pl.ds(1, count - 1)]
        plane_copy(sent, sent, me, other, r_s.at[c], r_r.at[c]).wait_send()

        @pl.when(sec == 0)
        def _():
            plane_copy(outb.at[c, 1, 0], ret.at[c, 0], me, 1, g_s.at[c], r_r.at[c]).wait_send()

        @pl.when(sec == 1)
        def _():
            sent = outb.at[c, :, 0]
            plane_copy(sent, sent, me, other, g_s.at[c], r_r.at[c]).wait_send()

        u_copy(c, others, me).wait_send()
    talk_copy.wait()

    level = partial_talk + trecv[...]
    level_scale = lax.rsqrt(jnp.mean(level * level, axis=1, keepdims=True) + 1e-06)
    level_out[...] = (level * level_scale * lgain[...]).astype(BF)


def head(hidden, level_normed, table, hidden_hbm, logits_hbm, logits, sems):
    hidden_copy = pltpu.make_async_copy(hidden, hidden_hbm, sems.at[0])
    hidden_copy.start()
    scores = jnp.dot(level_normed[...], table[...], preferred_element_type=F32)
    logits[...] = (scores / (table.shape[0] ** 0.5)).astype(BF)
    logits_copy = pltpu.make_async_copy(logits, logits_hbm, sems.at[1])
    logits_copy.start()
    hidden_copy.wait()
    logits_copy.wait()


def shards(
    tokens,
    routes,
    route_weight,
    moe_gain,
    expert_gate,
    expert_up,
    expert_down,
    talker_proj,
    codebook_table,
    level_gain,
    earlier_codes,
):
    rows, width = tokens.shape
    top = routes.shape[1]
    half, plane = width // 2, NY * NX
    ff = expert_gate.shape[2]
    vocabulary, talk_width = codebook_table.shape[1:]
    cw = half // CHUNKS
    span, stream = NZ * CAP, NZ * rows
    slots = plane * span
    chunk = (CHUNKS, plane, span, cw)
    by_core = (CHUNKS, 2, plane // 2, span, cw)
    dma = pltpu.SemaphoreType.DMA
    hbm = pl.BlockSpec(memory_space=pltpu.HBM)
    vmem = pl.BlockSpec(memory_space=pltpu.VMEM)
    operands = (
        tokens,
        routes.T,
        route_weight.T,
        moe_gain.reshape(1, width),
        expert_gate,
        expert_up,
        expert_down,
        talker_proj,
        codebook_table,
        level_gain,
        earlier_codes,
    )
    hidden, level_normed, table = pl.pallas_call(
        kernel,
        out_shape=(
            pltpu.VMEM((rows, half), BF),
            pltpu.VMEM((rows, talk_width), BF),
            pltpu.VMEM((talk_width, vocabulary), BF),
        ),
        in_specs=[hbm] * 11,
        out_specs=(vmem,) * 3,
        scratch_shapes=[
            pltpu.VMEM((vocabulary, talk_width), BF),
            pltpu.SMEM((rows,), jnp.int32),
            pltpu.VMEM((rows, width), BF),
            pltpu.VMEM((top, rows), jnp.int32),
            pltpu.VMEM((top, rows), F32),
            pltpu.VMEM((1, width), F32),
            pltpu.VMEM((1, talk_width), F32),
            pltpu.VMEM((width, 4 * ff), BF),
            pltpu.VMEM((2 * ff, width), BF),
            pltpu.VMEM((half, talk_width), BF),
            pltpu.VMEM((NZ, 2, top * rows), F32),
            pltpu.VMEM((CHUNKS, NZ, rows, cw), BF),
            pltpu.VMEM(chunk, BF),
            pltpu.VMEM(by_core, BF),
            pltpu.VMEM((slots // 2, 4 * ff), F32),
            pltpu.VMEM(by_core, BF),
            pltpu.VMEM(chunk, BF),
            pltpu.VMEM((CHUNKS, NZ, rows, cw), BF),
            pltpu.VMEM((CHUNKS, NZ, rows, cw), BF),
            pltpu.VMEM((2 * stream, slots), BF),
            pltpu.VMEM((rows, talk_width), F32),
            pltpu.VMEM((rows, talk_width), F32),
            pltpu.VMEM((rows, talk_width), F32),
            dma((11,)),
            dma,
            dma,
            dma((CHUNKS,)),
            dma((CHUNKS,)),
            dma((CHUNKS,)),
            dma((CHUNKS,)),
            dma((CHUNKS,)),
            dma((3,)),
            dma((3,)),
            dma((CHUNKS,)),
            dma((CHUNKS,)),
            dma((CHUNKS,)),
            dma((CHUNKS,)),
            dma((CHUNKS,)),
            dma,
            dma,
        ],
        compiler_params=pltpu.CompilerParams(
            collective_id=0, has_side_effects=True, vmem_limit_bytes=44 * 1024 * 1024
        ),
        name="expert_step",
    )(*[pltpu.with_memory_space_constraint(operand, pltpu.HBM) for operand in operands])
    hidden, logits = pl.pallas_call(
        head,
        out_shape=(
            jax.ShapeDtypeStruct((rows, half), BF),
            jax.ShapeDtypeStruct((rows, vocabulary), BF),
        ),
        in_specs=[vmem] * 3,
        out_specs=(hbm, hbm),
        scratch_shapes=[pltpu.VMEM((rows, vocabulary), BF), dma((2,))],
        compiler_params=pltpu.CompilerParams(vmem_limit_bytes=16 * 1024 * 1024),
        name="head",
    )(hidden, level_normed, table)
    return hidden, logits[:, None, :]


def solution(mesh):
    in_specs = (
        P("expert", None),
        P("expert", None),
        P("expert", None),
        P(),
        P("expert", None, "section"),
        P("expert", None, "section"),
        P("expert", "section", None),
        P("section", None),
        P("section", None, None),
        P("section", None),
        P("expert"),
    )
    out_specs = (P("expert", "section"), P("expert", "section", None))
    return jax.shard_map(shards, mesh=mesh, in_specs=in_specs, out_specs=out_specs, check_vma=False)
```
